32 devices in a mesh: tx: 4 (over z), ty: 8 (over y, x, core).
Axes of the slice: x: 2, y: 2, z: 4, core: 2. Of those that a mesh axis runs over, the one named last changes fastest.
Arguments:
- reduced_heat: float32 [8, 256, 512], P(None, 'ty', 'tx'), may hold values from 0.3 to 1.2
- substance_kind: int32 [8, 256, 512], P(None, 'ty', 'tx'), may hold values from 0 to 3
- moment_vector: float32 [3, 8, 256, 512], P(None, None, 'ty', 'tx'), may hold values from -4 to 4
- stray_tensor: float32 [6, 16, 512, 1024], P(None, 'tx', None, 'ty'), may hold values from -8 to 8
- diffusivity_nodes: float32 [16], replicated, may hold values from 0.5 to 1.5
- substance_factor: float32 [4], replicated, may hold values from 0.5 to 2
- ordering_threshold: float32 [4], replicated, may hold values from 0.7 to 1.1
- beam_transverse_spot: int32 [2], replicated, may hold values from 0 to 255
- beam_downtrack_spot: int32 [2], replicated, may hold values from 0 to 511
Outputs:
- warmed_state: float32 [8, 256, 512], P(None, 'ty', 'tx')
- demag_field: float32 [3, 8, 256, 512], P(None, None, 'ty', 'tx')
The draws below stay inside these ranges and needn't reach their ends.
All inputs are finite; a program needn't handle non-finite values.
Results may differ from the reference program's by a relative error of at most 0.00007.
Values sent between devices are 32-bit elements; how exact they have to be, the bound alone decides.
A program may use at most 128 MiB of HBM per device.

```python
import math
import jax
import jax.numpy as jnp
from jax import lax

CX = 128
CY = 32
FILM_SHEETS = 8
SWEEPS = 2
TABLE = 16
SUBSTANCE_KINDS = 4
DOWNTRACK_SITES = 512
TRANSVERSE_SITES = 256


def plant(values, rng, smallest, largest):
    longest = values.shape.index(max(values.shape))
    spots = []
    for shift in (0, 1):
        where = [jax.random.randint(jax.random.fold_in(rng, axis), (), 0, length) for axis, length in enumerate(values.shape)]
        where[longest] = (where[longest] + shift) % values.shape[longest]
        spots.append(tuple(where))
    return values.at[spots[0]].set(smallest).at[spots[1]].set(largest)


def levels(stream_key, shape, pieces, smallest, top_value):
    gain, own = 1.0, jax.random.fold_in(stream_key, 6)
    for axis_at, blocks in pieces:
        steps = jnp.exp(jax.random.uniform(jax.random.fold_in(own, axis_at), (blocks,), jnp.float32, smallest / len(pieces), top_value / len(pieces)))
        gain = gain * jnp.repeat(steps, shape[axis_at] // blocks).reshape([-1 if axis == axis_at else 1 for axis in range(len(shape))])
    return gain


def noise(own_key, shape, deviation, bound, cuts=(), held_as=jnp.bfloat16):
    factor_of = levels(own_key, shape, cuts, -0.22, 0.18) if cuts else 1.0
    values = jax.random.normal(own_key, shape, jnp.float32) * deviation * factor_of
    return jnp.minimum(jnp.maximum(values, -bound), bound).astype(held_as)


def setup_inputs(seed: int = 0) -> dict:
    keys = jax.random.split(jax.random.key(seed), 10)
    reduced_heat = jnp.clip(0.3 + 0.90000004 * jax.random.uniform(keys[0], (FILM_SHEETS, TRANSVERSE_SITES, DOWNTRACK_SITES), jnp.float32) ** levels(keys[0], (FILM_SHEETS, TRANSVERSE_SITES, DOWNTRACK_SITES), ((1, 8), (2, 4)), -0.2, 0.2), 0.3, 1.2)
    substance_kind = plant(jax.random.randint(keys[1], (FILM_SHEETS, TRANSVERSE_SITES, DOWNTRACK_SITES), 0, SUBSTANCE_KINDS), jax.random.fold_in(keys[1], 1), 0, SUBSTANCE_KINDS - 1).astype(jnp.int32)
    moment_vector = noise(keys[2], (3, FILM_SHEETS, TRANSVERSE_SITES, DOWNTRACK_SITES), 0.6, 4.0, ((2, 8), (3, 4)), jnp.float32)
    stray_tensor = noise(keys[3], (6, 2 * FILM_SHEETS, 2 * TRANSVERSE_SITES, 2 * DOWNTRACK_SITES), 2.0, 8.0, ((1, 4), (3, 8)), jnp.float32)
    diffusivity_nodes = jnp.clip(jnp.exp(jax.random.uniform(keys[4], (TABLE,), jnp.float32, math.log(0.5), math.log(1.5))), 0.5, 1.5)
    substance_factor = jnp.clip(jnp.exp(jax.random.uniform(keys[5], (SUBSTANCE_KINDS,), jnp.float32, math.log(0.5), math.log(2.0))), 0.5, 2.0)
    ordering_threshold = jnp.clip(jax.random.uniform(keys[6], (SUBSTANCE_KINDS,), jnp.float32, 0.7, 1.1), 0.7, 1.1)
    beam_transverse_spot = jax.random.randint(keys[7], (SWEEPS,), 0, TRANSVERSE_SITES).astype(jnp.int32)
    beam_downtrack_spot = jax.random.randint(keys[8], (SWEEPS,), 0, DOWNTRACK_SITES).astype(jnp.int32)
    return {"reduced_heat": reduced_heat, "substance_kind": substance_kind, "moment_vector": moment_vector, "stray_tensor": stray_tensor, "diffusivity_nodes": diffusivity_nodes, "substance_factor": substance_factor, "ordering_threshold": ordering_threshold, "beam_transverse_spot": beam_transverse_spot, "beam_downtrack_spot": beam_downtrack_spot}


AMBIENT_HEAT = 0.3
STEP_RATE = 0.05
LASER_POWER = 4.0
LASER_DEPTH = 4.0
ORDERING_SPREAD = 0.08
TABLE_LOW = 0.2
TABLE_SPAN = 1.6


def lookup_diffusivity(absolute, diffusivity_nodes):
    nodes = diffusivity_nodes.shape[0]
    spacing = TABLE_SPAN / (nodes - 1)
    total = jnp.zeros_like(absolute) + diffusivity_nodes[0]
    for index in range(nodes - 1):
        start_node = TABLE_LOW + index * spacing
        total = total + (diffusivity_nodes[index + 1] - diffusivity_nodes[index]) * jnp.clip((absolute - start_node) / spacing, 0.0, 1.0)
    return total


def per_particle(substance_kind, values):
    result = jnp.zeros(substance_kind.shape, jnp.float32)
    for grain in range(values.shape[0]):
        result = result + jnp.where(substance_kind == grain, values[grain], 0.0)
    return result


def laser_heating(row_ids, col_ids, sheet_indices, spot_row, spot_col, total_cols, col_width, row_width):
    along = ((col_ids - spot_col + total_cols // 2) % total_cols - total_cols // 2).astype(jnp.float32) / col_width
    across = (row_ids - spot_row).astype(jnp.float32) / row_width
    col_factor = jnp.exp(-0.5 * along * along)
    row_factor = jnp.exp(-0.5 * across * across)
    layer_factor = jnp.exp(-jnp.arange(sheet_indices, dtype=jnp.float32) / LASER_DEPTH)
    return layer_factor[:, None, None] * row_factor[None, :, None] * col_factor[None, None, :]


def heat_update(center, diffusivity, neighbours, heating):
    flux = jnp.zeros_like(center)
    for other_temp, other_cond in neighbours:
        flux = flux + 0.5 * (diffusivity + other_cond) * (other_temp - center)
    vertical = 0.5 * (diffusivity[1:] + diffusivity[:-1]) * (center[1:] - center[:-1])
    zero_layer = jnp.zeros_like(center[:1])
    flux = flux + jnp.concatenate([vertical, zero_layer], 0) - jnp.concatenate([zero_layer, vertical], 0)
    return center + STEP_RATE * (flux + LASER_POWER * heating)


def reference(reduced_heat, substance_kind, moment_vector, stray_tensor, diffusivity_nodes, substance_factor, ordering_threshold, beam_transverse_spot, beam_downtrack_spot):
    rotation_phase = reduced_heat - AMBIENT_HEAT
    site_multiplier = per_particle(substance_kind, substance_factor)
    row_ids = jnp.arange(TRANSVERSE_SITES, dtype=jnp.int32)
    col_ids = jnp.arange(DOWNTRACK_SITES, dtype=jnp.int32)
    for sweep in range(SWEEPS):
        diffusivity = site_multiplier * lookup_diffusivity(rotation_phase + AMBIENT_HEAT, diffusivity_nodes)
        padded_temp = jnp.pad(rotation_phase, ((0, 0), (1, 1), (0, 0)))
        padded_cond = jnp.pad(diffusivity, ((0, 0), (1, 1), (0, 0)))
        neighbours = [(jnp.roll(rotation_phase, 1, axis=2), jnp.roll(diffusivity, 1, axis=2)),
                      (jnp.roll(rotation_phase, -1, axis=2), jnp.roll(diffusivity, -1, axis=2)),
                      (padded_temp[:, :-2], padded_cond[:, :-2]),
                      (padded_temp[:, 2:], padded_cond[:, 2:])]
        heating = laser_heating(row_ids, col_ids, FILM_SHEETS, beam_transverse_spot[sweep], beam_downtrack_spot[sweep], DOWNTRACK_SITES, 0.5 * CX, 1.0 * CY)
        rotation_phase = heat_update(rotation_phase, diffusivity, neighbours, heating)
    warmed_state = rotation_phase + AMBIENT_HEAT
    proportion = jax.nn.sigmoid((per_particle(substance_kind, ordering_threshold) - warmed_state) / ORDERING_SPREAD)
    scaled = moment_vector * proportion[None]
    depth = jnp.fft.fft(jnp.pad(scaled, ((0, 0), (0, FILM_SHEETS), (0, 0), (0, 0))), axis=1)
    pairs = ((0, 3, 4), (3, 1, 5), (4, 5, 2))

    def one_layer(index):
        plane = lax.dynamic_index_in_dim(depth, index, 1, keepdims=False)
        taps = lax.dynamic_index_in_dim(stray_tensor, index, 1, keepdims=False)
        spectra = jnp.fft.fft2(jnp.pad(plane, ((0, 0), (0, TRANSVERSE_SITES), (0, DOWNTRACK_SITES))))
        fields = []
        for target in range(3):
            total = taps[pairs[target][0]] * spectra[0] + taps[pairs[target][1]] * spectra[1] + taps[pairs[target][2]] * spectra[2]
            fields.append(-total)
        return jnp.fft.ifft2(jnp.stack(fields))[:, :TRANSVERSE_SITES, :DOWNTRACK_SITES]

    planes = lax.map(one_layer, jnp.arange(2 * FILM_SHEETS, dtype=jnp.int32))
    demag = jnp.real(jnp.fft.ifft(planes, axis=0))[:FILM_SHEETS]
    demag_field = jnp.transpose(demag, (1, 0, 2, 3)).astype(jnp.float32)
    return warmed_state, demag_field
```

```python
import functools
import math

import jax
import jax.numpy as jnp
import ml_dtypes
import numpy as np
from jax import lax
from jax.experimental import pallas as pl
from jax.experimental.pallas import tpu as pltpu
from jax.sharding import PartitionSpec as P

SWEEPS = 2


AMBIENT_HEAT = 0.3
STEP_RATE = 0.05
LASER_POWER = 4.0
LASER_DEPTH = 4.0
ORDERING_SPREAD = 0.08
TABLE_LOW = 0.2
TABLE_SPAN = 1.6


def extended(value, sides, width, wrap):
    for axis, dim in sides:
        count, length = (lax.axis_size(axis), value.shape[dim])
        up = [(i, (i + 1) % count) for i in range(count if wrap else count - 1)]
        down = [(j, i) for i, j in up]
        last = lax.slice_in_dim(value, length - width, length, axis=dim)
        first = lax.slice_in_dim(value, 0, width, axis=dim)
        before = lax.ppermute(last, axis, up)
        after = lax.ppermute(first, axis, down)
        value = jnp.concatenate([before, value, after], axis=dim)
    return value


def lookup_diffusivity(absolute, diffusivity_nodes):
    nodes = diffusivity_nodes.shape[0]
    spacing = TABLE_SPAN / (nodes - 1)
    total = jnp.zeros_like(absolute) + diffusivity_nodes[0]
    for index in range(nodes - 1):
        start_node = TABLE_LOW + index * spacing
        total = total + (diffusivity_nodes[index + 1] - diffusivity_nodes[index]) * jnp.clip(
            (absolute - start_node) / spacing, 0.0, 1.0
        )
    return total


def per_particle(substance_kind, values):
    result = jnp.zeros(substance_kind.shape, jnp.float32)
    for grain in range(values.shape[0]):
        result = result + jnp.where(substance_kind == grain, values[grain], 0.0)
    return result


def laser_heating(
    row_ids, col_ids, sheet_indices, spot_row, spot_col, total_cols, col_width, row_width
):
    along = ((col_ids - spot_col + total_cols // 2) % total_cols - total_cols // 2).astype(
        jnp.float32
    ) / col_width
    across = (row_ids - spot_row).astype(jnp.float32) / row_width
    col_factor = jnp.exp(-0.5 * along * along)
    row_factor = jnp.exp(-0.5 * across * across)
    layer_factor = jnp.exp(-jnp.arange(sheet_indices, dtype=jnp.float32) / LASER_DEPTH)
    return layer_factor[:, None, None] * row_factor[None, :, None] * col_factor[None, None, :]


def heat_update(center, diffusivity, neighbours, heating):
    flux = jnp.zeros_like(center)
    for other_temp, other_cond in neighbours:
        flux = flux + 0.5 * (diffusivity + other_cond) * (other_temp - center)
    vertical = 0.5 * (diffusivity[1:] + diffusivity[:-1]) * (center[1:] - center[:-1])
    zero_layer = jnp.zeros_like(center[:1])
    flux = (
        flux
        + jnp.concatenate([vertical, zero_layer], 0)
        - jnp.concatenate([zero_layer, vertical], 0)
    )
    return center + STEP_RATE * (flux + LASER_POWER * heating)


MESH = pl.DeviceIdType.MESH
PAIRS = ((0, 3, 4), (3, 1, 5), (4, 5, 2))


def halves(table):
    high = table.astype(ml_dtypes.bfloat16)
    low = (table - high.astype(np.float64)).astype(ml_dtypes.bfloat16)
    return (high, low)


def angles(rows, cols, length):
    grid = np.outer(np.arange(rows), np.arange(cols)) % length
    return grid * (2.0 * math.pi / length)


def blocked_pair(angle, width):
    rows, cols = angle.shape
    cosine = np.cos(angle).reshape(rows, cols // width, width)
    sine = np.sin(angle).reshape(rows, cols // width, width)
    return np.concatenate([cosine, sine], axis=2).transpose(1, 0, 2)


def split(value):
    high = value.astype(jnp.bfloat16)
    return (high, (value - high.astype(jnp.float32)).astype(jnp.bfloat16))


def product(left_high, left_low, right_high, right_low):
    def dot(a, b):
        return jnp.dot(a, b, preferred_element_type=jnp.float32)

    return dot(left_high, right_high) + (dot(left_high, right_low) + dot(left_low, right_high))


def greet(tx, ty, ntx, nty):
    barrier = pltpu.get_barrier_semaphore()
    for step in range(1, ntx):
        pl.semaphore_signal(
            barrier, inc=1, device_id=(lax.rem(tx + step, ntx), ty), device_id_type=MESH
        )
    for step in range(1, nty):
        pl.semaphore_signal(
            barrier, inc=1, device_id=(tx, lax.rem(ty + step, nty)), device_id_type=MESH
        )
    pl.semaphore_wait(barrier, ntx + nty - 2)


def send_over(axis, step, part, source, target, sems, ntx, nty):
    tx, ty = lax.axis_index("tx"), lax.axis_index("ty")
    if axis == "tx":
        dest = lax.rem(tx + step, ntx)
        mine, device = tx, (dest, ty)
    else:
        dest = lax.rem(ty + step, nty)
        mine, device = ty, (tx, dest)
    return pltpu.make_async_remote_copy(
        src_ref=source.at[dest, part],
        dst_ref=target.at[mine, part],
        send_sem=sems[0].at[part, step],
        recv_sem=sems[1].at[part, step],
        device_id=device,
        device_id_type=MESH,
    )


def forward_kernel(
    ntx, nty, scaled, table_high, table_low, out, layered, gathered, left_high, left_low, blocks,
    tx_send, tx_recv, ty_send, ty_recv,
):
    tx, ty = lax.axis_index("tx"), lax.axis_index("ty")
    parts, sheets, rows, width = scaled.shape
    count = 2 * sheets
    own = count // ntx
    tx_sems, ty_sems = (tx_send, tx_recv), (ty_send, ty_recv)

    def over_tx(step, part):
        return send_over("tx", step, part, layered, gathered, tx_sems, ntx, nty)

    def over_ty(step, part):
        return send_over("ty", step, part, blocks, out, ty_sems, ntx, nty)

    def layer_part(part, carry):
        for freq in range(sheets + 1):
            real = jnp.zeros((rows, width), jnp.float32)
            imag = jnp.zeros((rows, width), jnp.float32)
            for sheet in range(sheets):
                value = scaled[part, sheet]
                angle = 2.0 * math.pi * (sheet * freq % count) / count
                real = real + value * math.cos(angle)
                imag = imag - value * math.sin(angle)
            layered[freq // own, part, 0, freq % own] = real
            layered[freq // own, part, 1, freq % own] = imag
            if 0 < freq < sheets:
                other = count - freq
                layered[other // own, part, 0, other % own] = real
                layered[other // own, part, 1, other % own] = -imag
        return carry

    lax.fori_loop(0, parts, layer_part, 0)
    greet(tx, ty, ntx, nty)
    for part in range(parts):
        for step in range(1, ntx):
            over_tx(step, part).start()

    def transform(block, part):
        result = product(left_high[...], left_low[...], table_high[block], table_low[block])
        half = own * rows
        real = result[:half, :width] + result[half:, width:]
        imag = result[half:, :width] - result[:half, width:]
        return real.reshape(own, rows, width), imag.reshape(own, rows, width)

    def transform_part(part, carry):
        for step in range(1, ntx):
            over_tx(step, part).wait_recv()
        gathered[tx, part] = layered[tx, part]
        for source in range(ntx):
            high, low = split(gathered[source, part].reshape(2 * own * rows, width))
            left_high[:, source * width : (source + 1) * width] = high
            left_low[:, source * width : (source + 1) * width] = low

        def one(step, inner):
            block = lax.rem(ty + step, nty)
            real, imag = transform(block, part)
            blocks[block, part, :, :, :width] = real
            blocks[block, part, :, :, width:] = imag
            over_ty(step, part).start()
            return inner

        lax.fori_loop(1, nty, one, 0)
        real, imag = transform(ty, part)
        out[ty, part, :, :, :width] = real
        out[ty, part, :, :, width:] = imag
        return carry

    lax.fori_loop(0, parts, transform_part, 0)
    for part in range(parts):
        for step in range(1, ntx):
            over_tx(step, part).wait_send()
        for step in range(1, nty):
            over_ty(step, part).wait()


def backward_kernel(
    ntx, nty, arrived, tensor_hbm, fwd_high, fwd_low, back_high, back_low, x_high_hbm, x_low_hbm,
    layers, out, tensor, x_high, x_low, spectra, field, returned, left_high, left_low, partial,
    landed, local_sem, ty_send, ty_recv, tx_send, tx_recv,
):
    tx, ty = lax.axis_index("tx"), lax.axis_index("ty")
    parts, own, rows = arrived.shape[1:4]
    width = arrived.shape[4] // 2
    total = nty * rows
    sheets = out.shape[1]
    tx_sems, ty_sems = (tx_send, tx_recv), (ty_send, ty_recv)
    loads = [
        pltpu.make_async_copy(tensor_hbm, tensor, local_sem.at[0]),
        pltpu.make_async_copy(x_high_hbm, x_high, local_sem.at[1]),
        pltpu.make_async_copy(x_low_hbm, x_low, local_sem.at[2]),
    ]
    for load in loads:
        load.start()

    def over_ty(step, part):
        return send_over("ty", step, part, field, returned, ty_sems, ntx, nty)

    def over_tx(step, part):
        return send_over("tx", step, part, partial, landed, tx_sems, ntx, nty)

    def forward_rows(index, carry):
        part, freq = index // own, index % own
        high, low = split(arrived[:, part, freq].reshape(total, 2 * width))
        result = product(fwd_high[...], fwd_low[...], high, low)
        half = 2 * total
        spectra[part, freq, :, :width] = result[:half, :width] + result[half:, width:]
        spectra[part, freq, :, width:] = result[:half, width:] - result[half:, :width]
        return carry

    lax.fori_loop(0, parts * own, forward_rows, 0)
    greet(tx, ty, ntx, nty)
    loads[0].wait()
    for part in range(parts):

        def back_rows(freq, carry):
            sides = []
            for side in range(2):
                lanes = slice(side * width, (side + 1) * width)
                sides.append(
                    tensor[PAIRS[part][0], freq] * spectra[0, freq, :, lanes]
                    + tensor[PAIRS[part][1], freq] * spectra[1, freq, :, lanes]
                    + tensor[PAIRS[part][2], freq] * spectra[2, freq, :, lanes]
                )
            high, low = split(jnp.concatenate(sides, axis=1))
            result = product(back_high[...], back_low[...], high, low)
            real = result[:total, :width] - result[total:, width:]
            imag = result[:total, width:] + result[total:, :width]
            field[:, part, 0, freq] = real.reshape(nty, rows, width)
            field[:, part, 1, freq] = imag.reshape(nty, rows, width)
            return carry

        lax.fori_loop(0, own, back_rows, 0)
        for step in range(1, nty):
            over_ty(step, part).start()
        returned[ty, part] = field[ty, part]
    loads[1].wait()
    loads[2].wait()

    def transform(block):
        result = product(left_high[...], left_low[...], x_high[block], x_low[block])
        half = own * rows
        real = result[:half, :width] - result[half:, width:]
        imag = result[:half, width:] + result[half:, :width]
        real, imag = real.reshape(own, rows, width), imag.reshape(own, rows, width)
        values = []
        for sheet in range(sheets):
            value = jnp.zeros((rows, width), jnp.float32)
            for freq in range(own):
                value = value + layers[tx * own + freq, 2 * sheet] * real[freq]
                value = value - layers[tx * own + freq, 2 * sheet + 1] * imag[freq]
            values.append(value)
        return values

    def inverse_part(part, carry):
        for step in range(1, nty):
            over_ty(step, part).wait_recv()
        for source in range(nty):
            high, low = split(returned[source, part].reshape(2 * own * rows, width))
            left_high[:, source * width : (source + 1) * width] = high
            left_low[:, source * width : (source + 1) * width] = low

        def one(step, inner):
            block = lax.rem(tx + step, ntx)
            for sheet, value in enumerate(transform(block)):
                partial[block, part, sheet] = value
            over_tx(step, part).start()
            return inner

        lax.fori_loop(1, ntx, one, 0)
        for sheet, value in enumerate(transform(tx)):
            landed[tx, part, sheet] = value
        return carry

    lax.fori_loop(0, parts, inverse_part, 0)
    for part in range(parts):
        for step in range(1, ntx):
            over_tx(step, part).wait_recv()
        total_field = landed[0, part]
        for source in range(1, ntx):
            total_field = total_field + landed[source, part]
        out[part] = total_field
    for part in range(parts):
        for step in range(1, nty):
            over_ty(step, part).wait_send()
        for step in range(1, ntx):
            over_tx(step, part).wait_send()


def vmem():
    return pl.BlockSpec(memory_space=pltpu.VMEM)


def params(identity):
    return pltpu.CompilerParams(
        collective_id=identity, has_side_effects=True, vmem_limit_bytes=60 * 1024 * 1024
    )


def spectra_over_rows(scaled, ntx, nty):
    parts, sheets, rows, width = scaled.shape
    own = 2 * sheets // ntx
    high, low = halves(blocked_pair(angles(ntx * width, nty * width, 2 * ntx * width), width))
    lines = 2 * own * rows
    dma = pltpu.SemaphoreType.DMA
    return pl.pallas_call(
        functools.partial(forward_kernel, ntx, nty),
        out_shape=jax.ShapeDtypeStruct((nty, parts, own, rows, 2 * width), jnp.float32),
        in_specs=[vmem()] * 3,
        out_specs=vmem(),
        scratch_shapes=[
            pltpu.VMEM((ntx, parts, 2, own, rows, width), jnp.float32),
            pltpu.VMEM((ntx, parts, 2, own, rows, width), jnp.float32),
            pltpu.VMEM((lines, ntx * width), jnp.bfloat16),
            pltpu.VMEM((lines, ntx * width), jnp.bfloat16),
            pltpu.VMEM((nty, parts, own, rows, 2 * width), jnp.float32),
            dma((parts, ntx)),
            dma((parts, ntx)),
            dma((parts, nty)),
            dma((parts, nty)),
        ],
        compiler_params=params(0),
        name="forward_spectra",
    )(scaled, high, low)


def field_from_spectra(arrived, stray_tensor, sheets, ntx, nty):
    parts, own, rows = arrived.shape[1:4]
    width = arrived.shape[4] // 2
    total, columns = nty * rows, ntx * width
    count = 2 * sheets
    forward = angles(2 * total, total, 2 * total)
    forward = halves(np.concatenate([np.cos(forward), np.sin(forward)], axis=0))
    back = angles(total, 2 * total, 2 * total)
    back = halves(np.concatenate([np.cos(back), np.sin(back)], axis=0))
    x_table = halves(blocked_pair(angles(nty * width, columns, 2 * columns), width))
    turn = angles(count, sheets, count)
    scale = -1.0 / (count * 2 * total * 2 * columns)
    layers = np.stack([np.cos(turn), np.sin(turn)], axis=2).reshape(count, 2 * sheets) * scale
    lines = 2 * own * rows
    dma = pltpu.SemaphoreType.DMA
    anywhere = pl.BlockSpec(memory_space=pl.ANY)
    return pl.pallas_call(
        functools.partial(backward_kernel, ntx, nty),
        out_shape=jax.ShapeDtypeStruct((parts, sheets, rows, width), jnp.float32),
        in_specs=[vmem(), anywhere, vmem(), vmem(), vmem(), vmem(), anywhere, anywhere]
        + [pl.BlockSpec(memory_space=pltpu.SMEM)],
        out_specs=vmem(),
        scratch_shapes=[
            pltpu.VMEM(stray_tensor.shape, jnp.float32),
            pltpu.VMEM(x_table[0].shape, jnp.bfloat16),
            pltpu.VMEM(x_table[1].shape, jnp.bfloat16),
            pltpu.VMEM((parts, own, 2 * total, 2 * width), jnp.float32),
            pltpu.VMEM((nty, parts, 2, own, rows, width), jnp.float32),
            pltpu.VMEM((nty, parts, 2, own, rows, width), jnp.float32),
            pltpu.VMEM((lines, nty * width), jnp.bfloat16),
            pltpu.VMEM((lines, nty * width), jnp.bfloat16),
            pltpu.VMEM((ntx, parts, sheets, rows, width), jnp.float32),
            pltpu.VMEM((ntx, parts, sheets, rows, width), jnp.float32),
            dma((3,)),
            dma((parts, nty)),
            dma((parts, nty)),
            dma((parts, ntx)),
            dma((parts, ntx)),
        ],
        compiler_params=params(1),
        name="field_return",
    )(arrived, stray_tensor, *forward, *back, *x_table, layers.astype(np.float32))


def local(
    reduced_heat,
    substance_kind,
    moment_vector,
    stray_tensor,
    diffusivity_nodes,
    substance_factor,
    ordering_threshold,
    beam_transverse_spot,
    beam_downtrack_spot,
):
    sheet_indices, downtrack_indices, transverse_indices = reduced_heat.shape
    total_rows = downtrack_indices * lax.axis_size("ty")
    total_cols = transverse_indices * lax.axis_size("tx")
    row_base = lax.axis_index("ty") * downtrack_indices
    col_base = lax.axis_index("tx") * transverse_indices
    rotation_phase = reduced_heat - AMBIENT_HEAT
    site_multiplier = per_particle(substance_kind, substance_factor)
    row_ids = row_base + jnp.arange(downtrack_indices, dtype=jnp.int32)
    col_ids = col_base + jnp.arange(transverse_indices, dtype=jnp.int32)
    for sweep in range(SWEEPS):
        diffusivity = site_multiplier * lookup_diffusivity(
            rotation_phase + AMBIENT_HEAT, diffusivity_nodes
        )
        fields = jnp.stack([rotation_phase, diffusivity])
        along = extended(fields, (("tx", 3),), 1, True)
        across = extended(fields, (("ty", 2),), 1, False)
        neighbours = [
            (along[0, :, :, :-2], along[1, :, :, :-2]),
            (along[0, :, :, 2:], along[1, :, :, 2:]),
            (across[0, :, :-2], across[1, :, :-2]),
            (across[0, :, 2:], across[1, :, 2:]),
        ]
        heating = laser_heating(
            row_ids,
            col_ids,
            sheet_indices,
            beam_transverse_spot[sweep],
            beam_downtrack_spot[sweep],
            total_cols,
            0.5 * transverse_indices,
            1.0 * downtrack_indices,
        )
        rotation_phase = heat_update(rotation_phase, diffusivity, neighbours, heating)
    warmed_state = rotation_phase + AMBIENT_HEAT
    proportion = jax.nn.sigmoid(
        (per_particle(substance_kind, ordering_threshold) - warmed_state) / ORDERING_SPREAD
    )
    scaled = moment_vector * proportion[None]
    ntx, nty = lax.axis_size("tx"), lax.axis_size("ty")
    arrived = spectra_over_rows(scaled, ntx, nty)
    demag_field = field_from_spectra(arrived, stray_tensor, sheet_indices, ntx, nty)
    return (warmed_state, demag_field)


def solution(mesh):
    in_specs = (
        P(None, "ty", "tx"),
        P(None, "ty", "tx"),
        P(None, None, "ty", "tx"),
        P(None, "tx", None, "ty"),
        P(),
        P(),
        P(),
        P(),
        P(),
    )
    out_specs = (P(None, "ty", "tx"), P(None, None, "ty", "tx"))
    return jax.shard_map(local, mesh=mesh, in_specs=in_specs, out_specs=out_specs, check_vma=False)
```

```python
import functools
import math

import jax
import jax.numpy as jnp
import ml_dtypes
import numpy as np
from jax import lax
from jax.experimental import pallas as pl
from jax.experimental.pallas import tpu as pltpu
from jax.sharding import PartitionSpec as P

SWEEPS = 2


AMBIENT_HEAT = 0.3
STEP_RATE = 0.05
LASER_POWER = 4.0
LASER_DEPTH = 4.0
ORDERING_SPREAD = 0.08
TABLE_LOW = 0.2
TABLE_SPAN = 1.6


MESH = pl.DeviceIdType.MESH
PAIRS = ((0, 3, 4), (3, 1, 5), (4, 5, 2))


def halves(table):
    high = table.astype(ml_dtypes.bfloat16)
    low = (table - high.astype(np.float64)).astype(ml_dtypes.bfloat16)
    return (high, low)


def angles(rows, cols, length):
    grid = np.outer(np.arange(rows), np.arange(cols)) % length
    return grid * (2.0 * math.pi / length)


def blocked_pair(angle, width):
    rows, cols = angle.shape
    cosine = np.cos(angle).reshape(rows, cols // width, width)
    sine = np.sin(angle).reshape(rows, cols // width, width)
    return np.concatenate([cosine, sine], axis=2).transpose(1, 0, 2)


def split(value):
    high = value.astype(jnp.bfloat16)
    return (high, (value - high.astype(jnp.float32)).astype(jnp.bfloat16))


def product(left_high, left_low, right_high, right_low):
    def dot(a, b):
        return jnp.dot(a, b, preferred_element_type=jnp.float32)

    return dot(left_high, right_high) + (dot(left_high, right_low) + dot(left_low, right_high))


def greet(tx, ty, ntx, nty):
    barrier = pltpu.get_barrier_semaphore()
    for step in range(1, ntx):
        pl.semaphore_signal(
            barrier, inc=1, device_id=(lax.rem(tx + step, ntx), ty), device_id_type=MESH
        )
    for step in range(1, nty):
        pl.semaphore_signal(
            barrier, inc=1, device_id=(tx, lax.rem(ty + step, nty)), device_id_type=MESH
        )
    pl.semaphore_wait(barrier, ntx + nty - 2)


def send_over(axis, step, part, source, target, sems, ntx, nty):
    tx, ty = lax.axis_index("tx"), lax.axis_index("ty")
    if axis == "tx":
        dest = lax.rem(tx + step, ntx)
        mine, device = tx, (dest, ty)
    else:
        dest = lax.rem(ty + step, nty)
        mine, device = ty, (tx, dest)
    return pltpu.make_async_remote_copy(
        src_ref=source.at[dest, part],
        dst_ref=target.at[mine, part],
        send_sem=sems[0].at[part, step],
        recv_sem=sems[1].at[part, step],
        device_id=device,
        device_id_type=MESH,
    )


def conductivity(absolute, multiplier, nodes):
    count = nodes.shape[0]
    spacing = TABLE_SPAN / (count - 1)
    total = jnp.zeros_like(absolute) + nodes[0]
    for index in range(count - 1):
        place = (absolute - (TABLE_LOW + index * spacing)) * (1.0 / spacing)
        total = total + (nodes[index + 1] - nodes[index]) * jnp.clip(place, 0.0, 1.0)
    return multiplier * total


def of_kind(kind, values):
    result = jnp.zeros(kind.shape, jnp.float32)
    for grain in range(values.shape[0]):
        result = result + jnp.where(kind == grain, values[grain], 0.0)
    return result


def laser_plane(rows, width, tx, ty, ntx, row_spot, col_spot):
    total = ntx * width
    row_ids = lax.broadcasted_iota(jnp.int32, (rows, width), 0) + ty * rows
    col_ids = lax.broadcasted_iota(jnp.int32, (rows, width), 1) + tx * width
    along = col_ids - col_spot + total // 2
    along = jnp.where(along < 0, along + total, along)
    along = jnp.where(along >= total, along - total, along) - total // 2
    along = along.astype(jnp.float32) * (1.0 / (0.5 * width))
    across = (row_ids - row_spot).astype(jnp.float32) * (1.0 / rows)
    return jnp.exp(-0.5 * across * across) * jnp.exp(-0.5 * along * along)


def heat_sweeps(
    ntx, nty, heat, kind, nodes, factor, row_spots, col_spots, rows_out, rows_in, cols_out, cols_in,
    edge_send, edge_recv,
):
    tx, ty = lax.axis_index("tx"), lax.axis_index("ty")
    sheets, rows, width = heat.shape
    flat, cube = (sheets * rows, width), (sheets, rows, width)
    lane = lax.broadcasted_iota(jnp.int32, cube, 2)
    line = lax.broadcasted_iota(jnp.int32, cube, 1)
    theta = heat[...] - AMBIENT_HEAT
    multiplier = of_kind(kind[...], factor)
    started = []
    for sweep in range(SWEEPS):
        cond = conductivity(theta + AMBIENT_HEAT, multiplier, nodes)
        pair = (theta, cond)
        for place, value in enumerate(pair):
            rows_out[sweep, 0, place] = value[:, 0, :]
            rows_out[sweep, 1, place] = value[:, rows - 1, :]
            turned = value.reshape(flat).T
            cols_out[sweep, 0, place : place + 1] = turned[:1]
            cols_out[sweep, 1, place : place + 1] = turned[width - 1 :]
        copies = []
        for side, shift in enumerate((-1, 1)):
            targets = (
                (cols_out, cols_in, (lax.rem(tx + shift + ntx, ntx), ty)),
                (rows_out, rows_in, (tx, lax.rem(ty + shift + nty, nty))),
            )
            for axis, (source, target, device) in enumerate(targets):
                copy = pltpu.make_async_remote_copy(
                    src_ref=source.at[sweep, side],
                    dst_ref=target.at[sweep, side],
                    send_sem=edge_send.at[sweep, side, axis],
                    recv_sem=edge_recv.at[sweep, side, axis],
                    device_id=device,
                    device_id_type=MESH,
                )
                copy.start()
                copies.append(copy)
        started += copies
        plane = laser_plane(rows, width, tx, ty, ntx, row_spots[sweep], col_spots[sweep])
        heating = jnp.stack([plane * math.exp(-sheet / LASER_DEPTH) for sheet in range(sheets)])
        vertical = 0.5 * (cond[1:] + cond[:-1]) * (theta[1:] - theta[:-1])
        zero_layer = jnp.zeros_like(theta[:1])
        flux = jnp.concatenate([vertical, zero_layer], 0) - jnp.concatenate(
            [zero_layer, vertical], 0
        )
        for copy in copies:
            copy.wait_recv()
        for side, shift in enumerate((-1, 1)):
            turned = cols_in[sweep, side].T
            edge = 0 if shift == 1 else width - 1
            other = []
            for place, value in enumerate(pair):
                moved = pltpu.roll(value.reshape(flat), shift % width, 1).reshape(cube)
                column = turned[:, place : place + 1].reshape(sheets, rows, 1)
                other.append(jnp.where(lane == edge, column, moved))
            flux = flux + 0.5 * (cond + other[1]) * (other[0] - theta)
            edge = 0 if shift == 1 else rows - 1
            inside = ty > 0 if shift == 1 else ty < nty - 1
            other = []
            for place, value in enumerate(pair):
                moved = pltpu.roll(value.reshape(flat), shift % flat[0], 0).reshape(cube)
                row = jnp.where(inside, rows_in[sweep, side, place], 0.0)
                other.append(jnp.where(line == edge, row[:, None, :], moved))
            flux = flux + 0.5 * (cond + other[1]) * (other[0] - theta)
        theta = theta + STEP_RATE * (flux + LASER_POWER * heating)
    return theta + AMBIENT_HEAT, started


def edge_scratch(sheets, rows, width):
    edge_rows = pltpu.VMEM((SWEEPS, 2, 2, sheets, width), jnp.float32)
    edge_cols = pltpu.VMEM((SWEEPS, 2, 8, sheets * rows), jnp.float32)
    sems = pltpu.SemaphoreType.DMA((SWEEPS, 2, 2))
    return [edge_rows, edge_rows, edge_cols, edge_cols, sems, sems]


def forward_kernel(
    ntx, nty, heat, kind, moment, nodes, factor, threshold, row_spots, col_spots, table_high,
    table_low, warmed, out, proportion, layered, gathered, left_high, left_low, blocks, rows_out,
    rows_in, cols_out, cols_in, edge_send, edge_recv, tx_send, tx_recv, ty_send, ty_recv,
):
    tx, ty = lax.axis_index("tx"), lax.axis_index("ty")
    parts, sheets, rows, width = moment.shape
    greet(tx, ty, ntx, nty)
    cols_out[...] = jnp.zeros_like(cols_out)
    state, edges = heat_sweeps(
        ntx, nty, heat, kind, nodes, factor, row_spots, col_spots, rows_out, rows_in, cols_out,
        cols_in, edge_send, edge_recv,
    )
    warmed[...] = state
    proportion[...] = jax.nn.sigmoid(
        (of_kind(kind[...], threshold) - state) * (1.0 / ORDERING_SPREAD)
    )
    count = 2 * sheets
    own = count // ntx
    tx_sems, ty_sems = (tx_send, tx_recv), (ty_send, ty_recv)

    def over_tx(step, part):
        return send_over("tx", step, part, layered, gathered, tx_sems, ntx, nty)

    def over_ty(step, part):
        return send_over("ty", step, part, blocks, out, ty_sems, ntx, nty)

    def layer_part(part, carry):
        for freq in range(sheets + 1):
            real = jnp.zeros((rows, width), jnp.float32)
            imag = jnp.zeros((rows, width), jnp.float32)
            for sheet in range(sheets):
                value = moment[part, sheet] * proportion[sheet]
                angle = 2.0 * math.pi * (sheet * freq % count) / count
                real = real + value * math.cos(angle)
                imag = imag - value * math.sin(angle)
            layered[freq // own, part, 0, freq % own] = real
            layered[freq // own, part, 1, freq % own] = imag
            if 0 < freq < sheets:
                other = count - freq
                layered[other // own, part, 0, other % own] = real
                layered[other // own, part, 1, other % own] = -imag
        return carry

    for part in range(parts):
        layer_part(part, 0)
        for step in range(1, ntx):
            over_tx(step, part).start()

    def transform(block, part):
        result = product(left_high[...], left_low[...], table_high[block], table_low[block])
        half = own * rows
        real = result[:half, :width] + result[half:, width:]
        imag = result[half:, :width] - result[:half, width:]
        return real.reshape(own, rows, width), imag.reshape(own, rows, width)

    def transform_part(part, carry):
        for step in range(1, ntx):
            over_tx(step, part).wait_recv()
        gathered[tx, part] = layered[tx, part]
        for source in range(ntx):
            high, low = split(gathered[source, part].reshape(2 * own * rows, width))
            left_high[:, source * width : (source + 1) * width] = high
            left_low[:, source * width : (source + 1) * width] = low

        def one(step, inner):
            block = lax.rem(ty + step, nty)
            real, imag = transform(block, part)
            blocks[block, part, :, :, :width] = real
            blocks[block, part, :, :, width:] = imag
            over_ty(step, part).start()
            return inner

        lax.fori_loop(1, nty, one, 0)
        real, imag = transform(ty, part)
        out[ty, part, :, :, :width] = real
        out[ty, part, :, :, width:] = imag
        return carry

    lax.fori_loop(0, parts, transform_part, 0)
    for edge in edges:
        edge.wait_send()
    for part in range(parts):
        for step in range(1, ntx):
            over_tx(step, part).wait_send()
        for step in range(1, nty):
            over_ty(step, part).wait()


def backward_kernel(
    ntx, nty, arrived, tensor_hbm, fwd_high, fwd_low, back_high, back_low, x_high_hbm, x_low_hbm,
    layers, out, tensor, x_high, x_low, spectra, field, returned, left_high, left_low, partial,
    landed, local_sem, ty_send, ty_recv, tx_send, tx_recv,
):
    tx, ty = lax.axis_index("tx"), lax.axis_index("ty")
    parts, own, rows = arrived.shape[1:4]
    width = arrived.shape[4] // 2
    total = nty * rows
    sheets = out.shape[1]
    tx_sems, ty_sems = (tx_send, tx_recv), (ty_send, ty_recv)
    loads = [
        pltpu.make_async_copy(tensor_hbm, tensor, local_sem.at[0]),
        pltpu.make_async_copy(x_high_hbm, x_high, local_sem.at[1]),
        pltpu.make_async_copy(x_low_hbm, x_low, local_sem.at[2]),
    ]
    for load in loads:
        load.start()

    def over_ty(step, part):
        return send_over("ty", step, part, field, returned, ty_sems, ntx, nty)

    def over_tx(step, part):
        return send_over("tx", step, part, partial, landed, tx_sems, ntx, nty)

    def forward_rows(index, carry):
        part, freq = index // own, index % own
        high, low = split(arrived[:, part, freq].reshape(total, 2 * width))
        result = product(fwd_high[...], fwd_low[...], high, low)
        half = 2 * total
        spectra[part, freq, :, :width] = result[:half, :width] + result[half:, width:]
        spectra[part, freq, :, width:] = result[:half, width:] - result[half:, :width]
        return carry

    lax.fori_loop(0, parts * own, forward_rows, 0)
    greet(tx, ty, ntx, nty)
    loads[0].wait()
    for part in range(parts):

        def back_rows(freq, carry):
            sides = []
            for side in range(2):
                lanes = slice(side * width, (side + 1) * width)
                sides.append(
                    tensor[PAIRS[part][0], freq] * spectra[0, freq, :, lanes]
                    + tensor[PAIRS[part][1], freq] * spectra[1, freq, :, lanes]
                    + tensor[PAIRS[part][2], freq] * spectra[2, freq, :, lanes]
                )
            high, low = split(jnp.concatenate(sides, axis=1))
            result = product(back_high[...], back_low[...], high, low)
            real = result[:total, :width] - result[total:, width:]
            imag = result[:total, width:] + result[total:, :width]
            field[:, part, 0, freq] = real.reshape(nty, rows, width)
            field[:, part, 1, freq] = imag.reshape(nty, rows, width)
            return carry

        lax.fori_loop(0, own, back_rows, 0)
        for step in range(1, nty):
            over_ty(step, part).start()
        returned[ty, part] = field[ty, part]
    loads[1].wait()
    loads[2].wait()

    def transform(block):
        result = product(left_high[...], left_low[...], x_high[block], x_low[block])
        half = own * rows
        real = result[:half, :width] - result[half:, width:]
        imag = result[:half, width:] + result[half:, :width]
        real, imag = real.reshape(own, rows, width), imag.reshape(own, rows, width)
        values = []
        for sheet in range(sheets):
            value = jnp.zeros((rows, width), jnp.float32)
            for freq in range(own):
                value = value + layers[tx * own + freq, 2 * sheet] * real[freq]
                value = value - layers[tx * own + freq, 2 * sheet + 1] * imag[freq]
            values.append(value)
        return values

    def inverse_part(part, carry):
        for step in range(1, nty):
            over_ty(step, part).wait_recv()
        for source in range(nty):
            high, low = split(returned[source, part].reshape(2 * own * rows, width))
            left_high[:, source * width : (source + 1) * width] = high
            left_low[:, source * width : (source + 1) * width] = low

        def one(step, inner):
            block = lax.rem(tx + step, ntx)
            for sheet, value in enumerate(transform(block)):
                partial[block, part, sheet] = value
            over_tx(step, part).start()
            return inner

        lax.fori_loop(1, ntx, one, 0)
        for sheet, value in enumerate(transform(tx)):
            landed[tx, part, sheet] = value
        return carry

    lax.fori_loop(0, parts, inverse_part, 0)
    for part in range(parts):
        for step in range(1, ntx):
            over_tx(step, part).wait_recv()
        total_field = landed[0, part]
        for source in range(1, ntx):
            total_field = total_field + landed[source, part]
        out[part] = total_field
    for part in range(parts):
        for step in range(1, nty):
            over_ty(step, part).wait_send()
        for step in range(1, ntx):
            over_tx(step, part).wait_send()


def vmem():
    return pl.BlockSpec(memory_space=pltpu.VMEM)


def params(identity):
    return pltpu.CompilerParams(
        collective_id=identity, has_side_effects=True, vmem_limit_bytes=60 * 1024 * 1024
    )


def spectra_over_rows(heat, kind, moment, scalars, ntx, nty):
    parts, sheets, rows, width = moment.shape
    own = 2 * sheets // ntx
    high, low = halves(blocked_pair(angles(ntx * width, nty * width, 2 * ntx * width), width))
    lines = 2 * own * rows
    dma = pltpu.SemaphoreType.DMA
    return pl.pallas_call(
        functools.partial(forward_kernel, ntx, nty),
        out_shape=(
            jax.ShapeDtypeStruct(heat.shape, jnp.float32),
            jax.ShapeDtypeStruct((nty, parts, own, rows, 2 * width), jnp.float32),
        ),
        in_specs=[vmem()] * 3
        + [pl.BlockSpec(memory_space=pltpu.SMEM)] * len(scalars)
        + [vmem()] * 2,
        out_specs=(vmem(), vmem()),
        scratch_shapes=[
            pltpu.VMEM((sheets, rows, width), jnp.float32),
            pltpu.VMEM((ntx, parts, 2, own, rows, width), jnp.float32),
            pltpu.VMEM((ntx, parts, 2, own, rows, width), jnp.float32),
            pltpu.VMEM((lines, ntx * width), jnp.bfloat16),
            pltpu.VMEM((lines, ntx * width), jnp.bfloat16),
            pltpu.VMEM((nty, parts, own, rows, 2 * width), jnp.float32),
            *edge_scratch(sheets, rows, width),
            dma((parts, ntx)),
            dma((parts, ntx)),
            dma((parts, nty)),
            dma((parts, nty)),
        ],
        compiler_params=params(0),
        name="forward_spectra",
    )(heat, kind, moment, *scalars, high, low)


def field_from_spectra(arrived, stray_tensor, sheets, ntx, nty):
    parts, own, rows = arrived.shape[1:4]
    width = arrived.shape[4] // 2
    total, columns = nty * rows, ntx * width
    count = 2 * sheets
    forward = angles(2 * total, total, 2 * total)
    forward = halves(np.concatenate([np.cos(forward), np.sin(forward)], axis=0))
    back = angles(total, 2 * total, 2 * total)
    back = halves(np.concatenate([np.cos(back), np.sin(back)], axis=0))
    x_table = halves(blocked_pair(angles(nty * width, columns, 2 * columns), width))
    turn = angles(count, sheets, count)
    scale = -1.0 / (count * 2 * total * 2 * columns)
    layers = np.stack([np.cos(turn), np.sin(turn)], axis=2).reshape(count, 2 * sheets) * scale
    lines = 2 * own * rows
    dma = pltpu.SemaphoreType.DMA
    anywhere = pl.BlockSpec(memory_space=pl.ANY)
    return pl.pallas_call(
        functools.partial(backward_kernel, ntx, nty),
        out_shape=jax.ShapeDtypeStruct((parts, sheets, rows, width), jnp.float32),
        in_specs=[vmem(), anywhere, vmem(), vmem(), vmem(), vmem(), anywhere, anywhere]
        + [pl.BlockSpec(memory_space=pltpu.SMEM)],
        out_specs=vmem(),
        scratch_shapes=[
            pltpu.VMEM(stray_tensor.shape, jnp.float32),
            pltpu.VMEM(x_table[0].shape, jnp.bfloat16),
            pltpu.VMEM(x_table[1].shape, jnp.bfloat16),
            pltpu.VMEM((parts, own, 2 * total, 2 * width), jnp.float32),
            pltpu.VMEM((nty, parts, 2, own, rows, width), jnp.float32),
            pltpu.VMEM((nty, parts, 2, own, rows, width), jnp.float32),
            pltpu.VMEM((lines, nty * width), jnp.bfloat16),
            pltpu.VMEM((lines, nty * width), jnp.bfloat16),
            pltpu.VMEM((ntx, parts, sheets, rows, width), jnp.float32),
            pltpu.VMEM((ntx, parts, sheets, rows, width), jnp.float32),
            dma((3,)),
            dma((parts, nty)),
            dma((parts, nty)),
            dma((parts, ntx)),
            dma((parts, ntx)),
        ],
        compiler_params=params(1),
        name="field_return",
    )(arrived, stray_tensor, *forward, *back, *x_table, layers.astype(np.float32))


def local(
    reduced_heat,
    substance_kind,
    moment_vector,
    stray_tensor,
    diffusivity_nodes,
    substance_factor,
    ordering_threshold,
    beam_transverse_spot,
    beam_downtrack_spot,
):
    ntx, nty = lax.axis_size("tx"), lax.axis_size("ty")
    scalars = (
        diffusivity_nodes,
        substance_factor,
        ordering_threshold,
        beam_transverse_spot,
        beam_downtrack_spot,
    )
    warmed_state, arrived = spectra_over_rows(
        reduced_heat, substance_kind, moment_vector, scalars, ntx, nty
    )
    demag_field = field_from_spectra(arrived, stray_tensor, reduced_heat.shape[0], ntx, nty)
    return (warmed_state, demag_field)


def solution(mesh):
    in_specs = (
        P(None, "ty", "tx"),
        P(None, "ty", "tx"),
        P(None, None, "ty", "tx"),
        P(None, "tx", None, "ty"),
        P(),
        P(),
        P(),
        P(),
        P(),
    )
    out_specs = (P(None, "ty", "tx"), P(None, None, "ty", "tx"))
    return jax.shard_map(local, mesh=mesh, in_specs=in_specs, out_specs=out_specs, check_vma=False)
```

```python
import functools
import math

import jax
import jax.numpy as jnp
import ml_dtypes
import numpy as np
from jax import lax
from jax.experimental import pallas as pl
from jax.experimental.pallas import tpu as pltpu
from jax.sharding import PartitionSpec as P

SWEEPS = 2


AMBIENT_HEAT = 0.3
STEP_RATE = 0.05
LASER_POWER = 4.0
LASER_DEPTH = 4.0
ORDERING_SPREAD = 0.08
TABLE_LOW = 0.2
TABLE_SPAN = 1.6


MESH = pl.DeviceIdType.MESH
AHEAD = 2
TABLE_BYTES = 16 * 1024 * 1024
PAIRS = ((0, 3, 4), (3, 1, 5), (4, 5, 2))


def halves(table):
    high = table.astype(ml_dtypes.bfloat16)
    low = (table - high.astype(np.float64)).astype(ml_dtypes.bfloat16)
    return (high, low)


def angles(rows, cols, length):
    grid = np.outer(np.arange(rows), np.arange(cols)) % length
    return grid * (2.0 * math.pi / length)


def blocked_pair(angle, width):
    rows, cols = angle.shape
    cosine = np.cos(angle).reshape(rows, cols // width, width)
    sine = np.sin(angle).reshape(rows, cols // width, width)
    return np.concatenate([cosine, sine], axis=2).transpose(1, 0, 2)


def split(value):
    high = value.astype(jnp.bfloat16)
    return (high, (value - high.astype(jnp.float32)).astype(jnp.bfloat16))


def product(left_high, left_low, right_high, right_low):
    def dot(a, b):
        return jnp.dot(a, b, preferred_element_type=jnp.float32)

    return dot(left_high, right_high) + (dot(left_high, right_low) + dot(left_low, right_high))


def greet(tx, ty, ntx, nty):
    barrier = pltpu.get_barrier_semaphore()
    for step in range(1, ntx):
        pl.semaphore_signal(
            barrier, inc=1, device_id=(lax.rem(tx + step, ntx), ty), device_id_type=MESH
        )
    for step in range(1, nty):
        pl.semaphore_signal(
            barrier, inc=1, device_id=(tx, lax.rem(ty + step, nty)), device_id_type=MESH
        )
    pl.semaphore_wait(barrier, ntx + nty - 2)


def send_over(axis, step, part, source, target, sems, ntx, nty):
    tx, ty = lax.axis_index("tx"), lax.axis_index("ty")
    if axis == "tx":
        dest = lax.rem(tx + step, ntx)
        mine, device = tx, (dest, ty)
    else:
        dest = lax.rem(ty + step, nty)
        mine, device = ty, (tx, dest)
    return pltpu.make_async_remote_copy(
        src_ref=source.at[dest, part],
        dst_ref=target.at[mine, part],
        send_sem=sems[0].at[part, step],
        recv_sem=sems[1].at[part, step],
        device_id=device,
        device_id_type=MESH,
    )


def conductivity(absolute, multiplier, nodes):
    count = nodes.shape[0]
    spacing = TABLE_SPAN / (count - 1)
    total = jnp.zeros_like(absolute) + nodes[0]
    for index in range(count - 1):
        place = (absolute - (TABLE_LOW + index * spacing)) * (1.0 / spacing)
        total = total + (nodes[index + 1] - nodes[index]) * jnp.clip(place, 0.0, 1.0)
    return multiplier * total


def of_kind(kind, values):
    result = jnp.zeros(kind.shape, jnp.float32)
    for grain in range(values.shape[0]):
        result = result + jnp.where(kind == grain, values[grain], 0.0)
    return result


def laser_plane(rows, width, tx, ty, ntx, row_spot, col_spot):
    total = ntx * width
    row_ids = lax.broadcasted_iota(jnp.int32, (rows, width), 0) + ty * rows
    col_ids = lax.broadcasted_iota(jnp.int32, (rows, width), 1) + tx * width
    along = col_ids - col_spot + total // 2
    along = jnp.where(along < 0, along + total, along)
    along = jnp.where(along >= total, along - total, along) - total // 2
    along = along.astype(jnp.float32) * (1.0 / (0.5 * width))
    across = (row_ids - row_spot).astype(jnp.float32) * (1.0 / rows)
    return jnp.exp(-0.5 * across * across) * jnp.exp(-0.5 * along * along)


def heat_sweeps(
    ntx, nty, heat, kind, nodes, factor, row_spots, col_spots, rows_out, rows_in, cols_out, cols_in,
    edge_send, edge_recv,
):
    tx, ty = lax.axis_index("tx"), lax.axis_index("ty")
    sheets, rows, width = heat.shape
    flat, cube = (sheets * rows, width), (sheets, rows, width)
    lane = lax.broadcasted_iota(jnp.int32, cube, 2)
    line = lax.broadcasted_iota(jnp.int32, cube, 1)
    theta = heat[...] - AMBIENT_HEAT
    multiplier = of_kind(kind[...], factor)
    started = []
    for sweep in range(SWEEPS):
        cond = conductivity(theta + AMBIENT_HEAT, multiplier, nodes)
        pair = (theta, cond)
        for place, value in enumerate(pair):
            rows_out[sweep, 0, place] = value[:, 0, :]
            rows_out[sweep, 1, place] = value[:, rows - 1, :]
            turned = value.reshape(flat).T
            cols_out[sweep, 0, place : place + 1] = turned[:1]
            cols_out[sweep, 1, place : place + 1] = turned[width - 1 :]
        copies = []
        for side, shift in enumerate((-1, 1)):
            targets = (
                (cols_out, cols_in, (lax.rem(tx + shift + ntx, ntx), ty)),
                (rows_out, rows_in, (tx, lax.rem(ty + shift + nty, nty))),
            )
            for axis, (source, target, device) in enumerate(targets):
                copy = pltpu.make_async_remote_copy(
                    src_ref=source.at[sweep, side],
                    dst_ref=target.at[sweep, side],
                    send_sem=edge_send.at[sweep, side, axis],
                    recv_sem=edge_recv.at[sweep, side, axis],
                    device_id=device,
                    device_id_type=MESH,
                )
                copy.start()
                copies.append(copy)
        started += copies
        plane = laser_plane(rows, width, tx, ty, ntx, row_spots[sweep], col_spots[sweep])
        heating = jnp.stack([plane * math.exp(-sheet / LASER_DEPTH) for sheet in range(sheets)])
        vertical = 0.5 * (cond[1:] + cond[:-1]) * (theta[1:] - theta[:-1])
        zero_layer = jnp.zeros_like(theta[:1])
        flux = jnp.concatenate([vertical, zero_layer], 0) - jnp.concatenate(
            [zero_layer, vertical], 0
        )
        for copy in copies:
            copy.wait_recv()
        for side, shift in enumerate((-1, 1)):
            turned = cols_in[sweep, side].T
            edge = 0 if shift == 1 else width - 1
            other = []
            for place, value in enumerate(pair):
                moved = pltpu.roll(value.reshape(flat), shift % width, 1).reshape(cube)
                column = turned[:, place : place + 1].reshape(sheets, rows, 1)
                other.append(jnp.where(lane == edge, column, moved))
            flux = flux + 0.5 * (cond + other[1]) * (other[0] - theta)
            edge = 0 if shift == 1 else rows - 1
            inside = ty > 0 if shift == 1 else ty < nty - 1
            other = []
            for place, value in enumerate(pair):
                moved = pltpu.roll(value.reshape(flat), shift % flat[0], 0).reshape(cube)
                row = jnp.where(inside, rows_in[sweep, side, place], 0.0)
                other.append(jnp.where(line == edge, row[:, None, :], moved))
            flux = flux + 0.5 * (cond + other[1]) * (other[0] - theta)
        theta = theta + STEP_RATE * (flux + LASER_POWER * heating)
    return theta + AMBIENT_HEAT, started


def edge_scratch(sheets, rows, width):
    edge_rows = pltpu.VMEM((SWEEPS, 2, 2, sheets, width), jnp.float32)
    edge_cols = pltpu.VMEM((SWEEPS, 2, 8, sheets * rows), jnp.float32)
    sems = pltpu.SemaphoreType.DMA((SWEEPS, 2, 2))
    return [edge_rows, edge_rows, edge_cols, edge_cols, sems, sems]


def forward_kernel(
    ntx, nty, heat, kind, moment, nodes, factor, threshold, row_spots, col_spots, table_high,
    table_low, warmed, out, proportion, layered, gathered, left_high, left_low, blocks, rows_out,
    rows_in, cols_out, cols_in, edge_send, edge_recv, tx_send, tx_recv, ty_send, ty_recv,
):
    tx, ty = lax.axis_index("tx"), lax.axis_index("ty")
    parts, sheets, rows, width = moment.shape
    greet(tx, ty, ntx, nty)
    cols_out[...] = jnp.zeros_like(cols_out)
    state, edges = heat_sweeps(
        ntx, nty, heat, kind, nodes, factor, row_spots, col_spots, rows_out, rows_in, cols_out,
        cols_in, edge_send, edge_recv,
    )
    warmed[...] = state
    proportion[...] = jax.nn.sigmoid(
        (of_kind(kind[...], threshold) - state) * (1.0 / ORDERING_SPREAD)
    )
    count = 2 * sheets
    own = count // ntx
    tx_sems, ty_sems = (tx_send, tx_recv), (ty_send, ty_recv)

    def over_tx(step, part):
        return send_over("tx", step, part, layered, gathered, tx_sems, ntx, nty)

    def over_ty(step, part):
        return send_over("ty", step, part, blocks, out, ty_sems, ntx, nty)

    def layer_part(part, carry):
        for freq in range(sheets + 1):
            real = jnp.zeros((rows, width), jnp.float32)
            imag = jnp.zeros((rows, width), jnp.float32)
            for sheet in range(sheets):
                value = moment[part, sheet] * proportion[sheet]
                angle = 2.0 * math.pi * (sheet * freq % count) / count
                real = real + value * math.cos(angle)
                imag = imag - value * math.sin(angle)
            layered[freq // own, part, 0, freq % own] = real
            layered[freq // own, part, 1, freq % own] = imag
            if 0 < freq < sheets:
                other = count - freq
                layered[other // own, part, 0, other % own] = real
                layered[other // own, part, 1, other % own] = -imag
        return carry

    for part in range(parts):
        layer_part(part, 0)
        for step in range(1, ntx):
            over_tx(step, part).start()

    def transform(block, part):
        result = product(left_high[...], left_low[...], table_high[block], table_low[block])
        half = own * rows
        real = result[:half, :width] + result[half:, width:]
        imag = result[half:, :width] - result[:half, width:]
        return real.reshape(own, rows, width), imag.reshape(own, rows, width)

    def transform_part(part, carry):
        for step in range(1, ntx):
            over_tx(step, part).wait_recv()
        gathered[tx, part] = layered[tx, part]
        for source in range(ntx):
            high, low = split(gathered[source, part].reshape(2 * own * rows, width))
            left_high[:, source * width : (source + 1) * width] = high
            left_low[:, source * width : (source + 1) * width] = low

        def one(step, inner):
            block = lax.rem(ty + step, nty)
            real, imag = transform(block, part)
            blocks[block, part, :, :, :width] = real
            blocks[block, part, :, :, width:] = imag
            over_ty(step, part).start()
            return inner

        lax.fori_loop(1, nty, one, 0)
        real, imag = transform(ty, part)
        out[ty, part, :, :, :width] = real
        out[ty, part, :, :, width:] = imag
        return carry

    lax.fori_loop(0, parts, transform_part, 0)
    for edge in edges:
        edge.wait_send()
    for part in range(parts):
        for step in range(1, ntx):
            over_tx(step, part).wait_send()
        for step in range(1, nty):
            over_ty(step, part).wait()


def backward_kernel(
    ntx, nty, arrived, tensor_hbm, fwd_high, fwd_low, back_high, back_low, x_high_hbm, x_low_hbm,
    layers, out, tensor, x_high, x_low, spectra, field, returned, left_high, left_low, partial,
    landed, local_sem, ty_send, ty_recv, tx_send, tx_recv,
):
    tx, ty = lax.axis_index("tx"), lax.axis_index("ty")
    parts, own, rows = arrived.shape[1:4]
    width = arrived.shape[4] // 2
    total = nty * rows
    sheets = out.shape[1]
    tx_sems, ty_sems = (tx_send, tx_recv), (ty_send, ty_recv)
    loads = [
        pltpu.make_async_copy(tensor_hbm, tensor, local_sem.at[0]),
        pltpu.make_async_copy(x_high_hbm, x_high, local_sem.at[1]),
        pltpu.make_async_copy(x_low_hbm, x_low, local_sem.at[2]),
    ]
    for load in loads:
        load.start()

    def over_ty(step, part):
        return send_over("ty", step, part, field, returned, ty_sems, ntx, nty)

    def over_tx(step, part):
        return send_over("tx", step, part, partial, landed, tx_sems, ntx, nty)

    def forward_rows(index, carry):
        part, freq = index // own, index % own
        high, low = split(arrived[:, part, freq].reshape(total, 2 * width))
        result = product(fwd_high[...], fwd_low[...], high, low)
        half = 2 * total
        spectra[part, freq, :, :width] = result[:half, :width] + result[half:, width:]
        spectra[part, freq, :, width:] = result[:half, width:] - result[half:, :width]
        return carry

    lax.fori_loop(0, parts * own, forward_rows, 0)
    greet(tx, ty, ntx, nty)
    loads[0].wait()
    for part in range(parts):

        def back_rows(freq, carry):
            sides = []
            for side in range(2):
                lanes = slice(side * width, (side + 1) * width)
                sides.append(
                    tensor[PAIRS[part][0], freq] * spectra[0, freq, :, lanes]
                    + tensor[PAIRS[part][1], freq] * spectra[1, freq, :, lanes]
                    + tensor[PAIRS[part][2], freq] * spectra[2, freq, :, lanes]
                )
            high, low = split(jnp.concatenate(sides, axis=1))
            result = product(back_high[...], back_low[...], high, low)
            real = result[:total, :width] - result[total:, width:]
            imag = result[:total, width:] + result[total:, :width]
            field[:, part, 0, freq] = real.reshape(nty, rows, width)
            field[:, part, 1, freq] = imag.reshape(nty, rows, width)
            return carry

        lax.fori_loop(0, own, back_rows, 0)
        for step in range(1, nty):
            over_ty(step, part).start()
        returned[ty, part] = field[ty, part]
    loads[1].wait()
    loads[2].wait()

    def transform(block):
        result = product(left_high[...], left_low[...], x_high[block], x_low[block])
        half = own * rows
        real = result[:half, :width] - result[half:, width:]
        imag = result[:half, width:] + result[half:, :width]
        real, imag = real.reshape(own, rows, width), imag.reshape(own, rows, width)
        values = []
        for sheet in range(sheets):
            value = jnp.zeros((rows, width), jnp.float32)
            for freq in range(own):
                value = value + layers[tx * own + freq, 2 * sheet] * real[freq]
                value = value - layers[tx * own + freq, 2 * sheet + 1] * imag[freq]
            values.append(value)
        return values

    def inverse_part(part, carry):
        for step in range(1, nty):
            over_ty(step, part).wait_recv()
        for source in range(nty):
            high, low = split(returned[source, part].reshape(2 * own * rows, width))
            left_high[:, source * width : (source + 1) * width] = high
            left_low[:, source * width : (source + 1) * width] = low

        def one(step, inner):
            block = lax.rem(tx + step, ntx)
            for sheet, value in enumerate(transform(block)):
                partial[block, part, sheet] = value
            over_tx(step, part).start()
            return inner

        lax.fori_loop(1, ntx, one, 0)
        for sheet, value in enumerate(transform(tx)):
            landed[tx, part, sheet] = value
        return carry

    lax.fori_loop(0, parts, inverse_part, 0)
    for part in range(parts):
        for step in range(1, ntx):
            over_tx(step, part).wait_recv()
        total_field = landed[0, part]
        for source in range(1, ntx):
            total_field = total_field + landed[source, part]
        out[part] = total_field
    for part in range(parts):
        for step in range(1, nty):
            over_ty(step, part).wait_send()
        for step in range(1, ntx):
            over_tx(step, part).wait_send()


def vmem():
    return pl.BlockSpec(memory_space=pltpu.VMEM)


def params(identity):
    return pltpu.CompilerParams(
        collective_id=identity, has_side_effects=True, vmem_limit_bytes=60 * 1024 * 1024
    )


def spectra_over_rows(heat, kind, moment, scalars, ntx, nty):
    parts, sheets, rows, width = moment.shape
    own = 2 * sheets // ntx
    high, low = halves(blocked_pair(angles(ntx * width, nty * width, 2 * ntx * width), width))
    lines = 2 * own * rows
    dma = pltpu.SemaphoreType.DMA
    return pl.pallas_call(
        functools.partial(forward_kernel, ntx, nty),
        out_shape=(
            jax.ShapeDtypeStruct(heat.shape, jnp.float32),
            jax.ShapeDtypeStruct((nty, parts, own, rows, 2 * width), jnp.float32),
        ),
        in_specs=[vmem()] * 3
        + [pl.BlockSpec(memory_space=pltpu.SMEM)] * len(scalars)
        + [vmem()] * 2,
        out_specs=(vmem(), vmem()),
        scratch_shapes=[
            pltpu.VMEM((sheets, rows, width), jnp.float32),
            pltpu.VMEM((ntx, parts, 2, own, rows, width), jnp.float32),
            pltpu.VMEM((ntx, parts, 2, own, rows, width), jnp.float32),
            pltpu.VMEM((lines, ntx * width), jnp.bfloat16),
            pltpu.VMEM((lines, ntx * width), jnp.bfloat16),
            pltpu.VMEM((nty, parts, own, rows, 2 * width), jnp.float32),
            *edge_scratch(sheets, rows, width),
            dma((parts, ntx)),
            dma((parts, ntx)),
            dma((parts, nty)),
            dma((parts, nty)),
        ],
        compiler_params=params(0),
        name="forward_spectra",
    )(heat, kind, moment, *scalars, high, low)


def field_from_spectra(arrived, stray_tensor, sheets, ntx, nty):
    parts, own, rows = arrived.shape[1:4]
    width = arrived.shape[4] // 2
    total, columns = nty * rows, ntx * width
    count = 2 * sheets
    forward = angles(2 * total, total, 2 * total)
    forward = halves(np.concatenate([np.cos(forward), np.sin(forward)], axis=0))
    back = angles(total, 2 * total, 2 * total)
    back = halves(np.concatenate([np.cos(back), np.sin(back)], axis=0))
    x_table = halves(blocked_pair(angles(nty * width, columns, 2 * columns), width))
    turn = angles(count, sheets, count)
    scale = -1.0 / (count * 2 * total * 2 * columns)
    layers = np.stack([np.cos(turn), np.sin(turn)], axis=2).reshape(count, 2 * sheets) * scale
    lines = 2 * own * rows
    dma = pltpu.SemaphoreType.DMA
    anywhere = pl.BlockSpec(memory_space=pl.ANY)
    return pl.pallas_call(
        functools.partial(backward_kernel, ntx, nty),
        out_shape=jax.ShapeDtypeStruct((parts, sheets, rows, width), jnp.float32),
        in_specs=[vmem(), anywhere, vmem(), vmem(), vmem(), vmem(), anywhere, anywhere]
        + [pl.BlockSpec(memory_space=pltpu.SMEM)],
        out_specs=vmem(),
        scratch_shapes=[
            pltpu.VMEM(stray_tensor.shape, jnp.float32),
            pltpu.VMEM(x_table[0].shape, jnp.bfloat16),
            pltpu.VMEM(x_table[1].shape, jnp.bfloat16),
            pltpu.VMEM((parts, own, 2 * total, 2 * width), jnp.float32),
            pltpu.VMEM((nty, parts, 2, own, rows, width), jnp.float32),
            pltpu.VMEM((nty, parts, 2, own, rows, width), jnp.float32),
            pltpu.VMEM((lines, nty * width), jnp.bfloat16),
            pltpu.VMEM((lines, nty * width), jnp.bfloat16),
            pltpu.VMEM((ntx, parts, sheets, rows, width), jnp.float32),
            pltpu.VMEM((ntx, parts, sheets, rows, width), jnp.float32),
            dma((3,)),
            dma((parts, nty)),
            dma((parts, nty)),
            dma((parts, ntx)),
            dma((parts, ntx)),
        ],
        compiler_params=params(1),
        name="field_return",
    )(arrived, stray_tensor, *forward, *back, *x_table, layers.astype(np.float32))


def whole_kernel(
    ntx, nty, heat, kind, moment, nodes, factor, threshold, row_spots, col_spots, fwd_high, fwd_low,
    back_high, back_low, tensor_hbm, to_high_hbm, to_low_hbm, from_high_hbm, from_low_hbm,
    warmed, out, proportion, layered, gathered, blocks, arrived, spectra, field, returned, partial,
    landed, tensor, to_high, to_low, from_high, from_low, along_high, along_low, inverse_high,
    inverse_low, rows_out, rows_in, cols_out, cols_in, edge_send, edge_recv, local_sem, tx_send,
    tx_recv, ty_send, ty_recv, ty_back_send, ty_back_recv, tx_back_send, tx_back_recv,
):
    tx, ty = lax.axis_index("tx"), lax.axis_index("ty")
    parts, sheets, rows, width = moment.shape
    count = 2 * sheets
    own = count // ntx
    total = nty * rows
    half = parts * rows
    loads = [
        pltpu.make_async_copy(source, target, local_sem.at[index])
        for index, (source, target) in enumerate(
            (
                (to_high_hbm, to_high),
                (to_low_hbm, to_low),
                (tensor_hbm, tensor),
                (from_high_hbm, from_high),
                (from_low_hbm, from_low),
            )
        )
    ]
    for load in loads:
        load.start()

    def tx_copy(step, freq):
        sems = (tx_send, tx_recv)
        return send_over("tx", step, freq, layered, gathered, sems, ntx, nty)

    def ty_copy(step, freq):
        return send_over("ty", step, freq, blocks, arrived, (ty_send, ty_recv), ntx, nty)

    def ty_return(step, freq):
        sems = (ty_back_send, ty_back_recv)
        return send_over("ty", step, freq, field, returned, sems, ntx, nty)

    def tx_return(step, freq):
        sems = (tx_back_send, tx_back_recv)
        return send_over("tx", step, freq, partial, landed, sems, ntx, nty)

    def start_all(copy, size, freq):
        for step in range(1, size):
            copy(step, freq).start()

    def await_all(copy, size, freq):
        for step in range(1, size):
            copy(step, freq).wait_recv()

    greet(tx, ty, ntx, nty)
    cols_out[...] = jnp.zeros_like(cols_out)
    state, edges = heat_sweeps(
        ntx, nty, heat, kind, nodes, factor, row_spots, col_spots, rows_out, rows_in, cols_out,
        cols_in, edge_send, edge_recv,
    )
    warmed[...] = state
    proportion[...] = jax.nn.sigmoid(
        (of_kind(kind[...], threshold) - state) * (1.0 / ORDERING_SPREAD)
    )

    def layer_spectra(freqs):
        def layer_part(part, carry):
            values = [moment[part, sheet] * proportion[sheet] for sheet in range(sheets)]
            for freq in freqs:
                real = jnp.zeros((rows, width), jnp.float32)
                imag = jnp.zeros((rows, width), jnp.float32)
                for sheet in range(sheets):
                    angle = 2.0 * math.pi * (sheet * freq % count) / count
                    real = real + values[sheet] * math.cos(angle)
                    imag = imag - values[sheet] * math.sin(angle)
                layered[freq // own, freq % own, 0, part] = real
                layered[freq // own, freq % own, 1, part] = imag
                if 0 < freq < sheets:
                    other = count - freq
                    layered[other // own, other % own, 0, part] = real
                    layered[other // own, other % own, 1, part] = -imag
            return carry

        lax.fori_loop(0, parts, layer_part, 0)

    ready = set()
    for freq in range(own):
        needed = []
        for line in range(sheets + 1):
            if line not in ready and freq in (line % own, (count - line) % own):
                needed.append(line)
        if needed:
            layer_spectra(needed)
            ready.update(needed)
        if freq < AHEAD:
            start_all(tx_copy, ntx, freq)

    def assemble(source, freq, size, high_ref, low_ref):
        for index in range(size):
            high, low = split(source[index, freq].reshape(2 * half, width))
            high_ref[:, index * width : (index + 1) * width] = high
            low_ref[:, index * width : (index + 1) * width] = low

    def along(block):
        result = product(along_high[...], along_low[...], to_high[block], to_low[block])
        real = result[:half, :width] + result[half:, width:]
        imag = result[half:, :width] - result[:half, width:]
        return real.reshape(parts, rows, width), imag.reshape(parts, rows, width)

    def forward_columns(freq):
        await_all(tx_copy, ntx, freq)
        if freq + AHEAD < own:
            start_all(tx_copy, ntx, freq + AHEAD)
        gathered[tx, freq] = layered[tx, freq]
        assemble(gathered, freq, ntx, along_high, along_low)
        if freq == 0:
            loads[0].wait()
            loads[1].wait()

        def one(step, carry):
            block = lax.rem(ty + step, nty)
            real, imag = along(block)
            blocks[block, freq, :, :, :width] = real
            blocks[block, freq, :, :, width:] = imag
            ty_copy(step, freq).start()
            return carry

        lax.fori_loop(1, nty, one, 0)
        real, imag = along(ty)
        arrived[ty, freq, :, :, :width] = real
        arrived[ty, freq, :, :, width:] = imag

    def through_rows(freq):
        await_all(ty_copy, nty, freq)

        def forward_rows(part, carry):
            high, low = split(arrived[:, freq, part].reshape(total, 2 * width))
            result = product(fwd_high[...], fwd_low[...], high, low)
            top = 2 * total
            spectra[part, :, :width] = result[:top, :width] + result[top:, width:]
            spectra[part, :, width:] = result[:top, width:] - result[top:, :width]
            return carry

        lax.fori_loop(0, parts, forward_rows, 0)
        if freq == 0:
            loads[2].wait()
        for part in range(parts):
            sides = []
            for side in range(2):
                lanes = slice(side * width, (side + 1) * width)
                sides.append(
                    tensor[PAIRS[part][0], freq] * spectra[0, :, lanes]
                    + tensor[PAIRS[part][1], freq] * spectra[1, :, lanes]
                    + tensor[PAIRS[part][2], freq] * spectra[2, :, lanes]
                )
            high, low = split(jnp.concatenate(sides, axis=1))
            result = product(back_high[...], back_low[...], high, low)
            real = result[:total, :width] - result[total:, width:]
            imag = result[:total, width:] + result[total:, :width]
            field[:, freq, 0, part] = real.reshape(nty, rows, width)
            field[:, freq, 1, part] = imag.reshape(nty, rows, width)
        start_all(ty_return, nty, freq)
        returned[ty, freq] = field[ty, freq]

    def inverse(block):
        result = product(inverse_high[...], inverse_low[...], from_high[block], from_low[block])
        real = result[:half, :width] - result[half:, width:]
        imag = result[:half, width:] + result[half:, :width]
        return real.reshape(parts, rows, width), imag.reshape(parts, rows, width)

    def inverse_columns(freq):
        await_all(ty_return, nty, freq)
        assemble(returned, freq, nty, inverse_high, inverse_low)
        if freq == 0:
            loads[3].wait()
            loads[4].wait()

        def one(step, carry):
            block = lax.rem(tx + step, ntx)
            partial[block, freq, 0], partial[block, freq, 1] = inverse(block)
            tx_return(step, freq).start()
            return carry

        lax.fori_loop(1, ntx, one, 0)
        landed[tx, freq, 0], landed[tx, freq, 1] = inverse(tx)

    for turn in range(own + 3):
        if turn < own:
            forward_columns(turn)
        if 0 <= turn - 1 < own:
            through_rows(turn - 1)
        if 0 <= turn - 3 < own:
            inverse_columns(turn - 3)

    scale = -1.0 / (count * 2 * total * 2 * ntx * width)
    for freq in range(own):
        await_all(tx_return, ntx, freq)

        def back_layers(part, carry):
            for sheet in range(sheets):
                value = jnp.zeros((rows, width), jnp.float32) if freq == 0 else out[part, sheet]
                for source in range(ntx):
                    line = source * own + freq
                    angle = 2.0 * math.pi * (sheet * line % count) / count
                    value = value + landed[source, freq, 0, part] * (scale * math.cos(angle))
                    value = value - landed[source, freq, 1, part] * (scale * math.sin(angle))
                out[part, sheet] = value
            return carry

        lax.fori_loop(0, parts, back_layers, 0)

    for edge in edges:
        edge.wait_send()
    for freq in range(own):
        for copy, size in ((tx_copy, ntx), (ty_copy, nty), (ty_return, nty), (tx_return, ntx)):
            for step in range(1, size):
                copy(step, freq).wait_send()


def everything(heat, kind, moment, stray_tensor, scalars, ntx, nty):
    parts, sheets, rows, width = moment.shape
    own = 2 * sheets // ntx
    total, columns = nty * rows, ntx * width
    forward = angles(2 * total, total, 2 * total)
    forward = halves(np.concatenate([np.cos(forward), np.sin(forward)], axis=0))
    back = angles(total, 2 * total, 2 * total)
    back = halves(np.concatenate([np.cos(back), np.sin(back)], axis=0))
    to_table = halves(blocked_pair(angles(columns, nty * width, 2 * columns), width))
    from_table = halves(blocked_pair(angles(nty * width, columns, 2 * columns), width))
    lines = 2 * parts * rows
    dma = pltpu.SemaphoreType.DMA
    anywhere = pl.BlockSpec(memory_space=pl.ANY)
    over_tx = pltpu.VMEM((ntx, own, 2, parts, rows, width), jnp.float32)
    over_ty = pltpu.VMEM((nty, own, parts, rows, 2 * width), jnp.float32)
    back_ty = pltpu.VMEM((nty, own, 2, parts, rows, width), jnp.float32)
    return pl.pallas_call(
        functools.partial(whole_kernel, ntx, nty),
        out_shape=(
            jax.ShapeDtypeStruct(heat.shape, jnp.float32),
            jax.ShapeDtypeStruct(moment.shape, jnp.float32),
        ),
        in_specs=[vmem()] * 3
        + [pl.BlockSpec(memory_space=pltpu.SMEM)] * len(scalars)
        + [vmem()] * 4
        + [anywhere] * 5,
        out_specs=(vmem(), vmem()),
        scratch_shapes=[
            pltpu.VMEM((sheets, rows, width), jnp.float32),
            over_tx,
            over_tx,
            over_ty,
            over_ty,
            pltpu.VMEM((parts, 2 * total, 2 * width), jnp.float32),
            back_ty,
            back_ty,
            over_tx,
            over_tx,
            pltpu.VMEM(stray_tensor.shape, jnp.float32),
            pltpu.VMEM(to_table[0].shape, jnp.bfloat16),
            pltpu.VMEM(to_table[1].shape, jnp.bfloat16),
            pltpu.VMEM(from_table[0].shape, jnp.bfloat16),
            pltpu.VMEM(from_table[1].shape, jnp.bfloat16),
            pltpu.VMEM((lines, columns), jnp.bfloat16),
            pltpu.VMEM((lines, columns), jnp.bfloat16),
            pltpu.VMEM((lines, nty * width), jnp.bfloat16),
            pltpu.VMEM((lines, nty * width), jnp.bfloat16),
            *edge_scratch(sheets, rows, width),
            dma((5,)),
            dma((own, ntx)),
            dma((own, ntx)),
            dma((own, nty)),
            dma((own, nty)),
            dma((own, nty)),
            dma((own, nty)),
            dma((own, ntx)),
            dma((own, ntx)),
        ],
        compiler_params=params(2),
        name="demagnetize",
    )(heat, kind, moment, *scalars, *forward, *back, stray_tensor, *to_table, *from_table)


def local(
    reduced_heat,
    substance_kind,
    moment_vector,
    stray_tensor,
    diffusivity_nodes,
    substance_factor,
    ordering_threshold,
    beam_transverse_spot,
    beam_downtrack_spot,
):
    ntx, nty = lax.axis_size("tx"), lax.axis_size("ty")
    scalars = (
        diffusivity_nodes,
        substance_factor,
        ordering_threshold,
        beam_transverse_spot,
        beam_downtrack_spot,
    )
    if 16 * ntx * nty * reduced_heat.shape[2] ** 2 <= TABLE_BYTES:
        return everything(
            reduced_heat, substance_kind, moment_vector, stray_tensor, scalars, ntx, nty
        )
    warmed_state, arrived = spectra_over_rows(
        reduced_heat, substance_kind, moment_vector, scalars, ntx, nty
    )
    demag_field = field_from_spectra(arrived, stray_tensor, reduced_heat.shape[0], ntx, nty)
    return (warmed_state, demag_field)


def solution(mesh):
    in_specs = (
        P(None, "ty", "tx"),
        P(None, "ty", "tx"),
        P(None, None, "ty", "tx"),
        P(None, "tx", None, "ty"),
        P(),
        P(),
        P(),
        P(),
        P(),
    )
    out_specs = (P(None, "ty", "tx"), P(None, None, "ty", "tx"))
    return jax.shard_map(local, mesh=mesh, in_specs=in_specs, out_specs=out_specs, check_vma=False)
```

```python
import functools
import math

import jax
import jax.numpy as jnp
import ml_dtypes
import numpy as np
from jax import lax
from jax.experimental import pallas as pl
from jax.experimental.pallas import tpu as pltpu
from jax.sharding import PartitionSpec as P

SWEEPS = 2


AMBIENT_HEAT = 0.3
STEP_RATE = 0.05
LASER_POWER = 4.0
LASER_DEPTH = 4.0
ORDERING_SPREAD = 0.08
TABLE_LOW = 0.2
TABLE_SPAN = 1.6


MESH = pl.DeviceIdType.MESH
AHEAD = 2
TABLE_BYTES = 16 * 1024 * 1024
PAIRS = ((0, 3, 4), (3, 1, 5), (4, 5, 2))


def halves(table):
    high = table.astype(ml_dtypes.bfloat16)
    low = (table - high.astype(np.float64)).astype(ml_dtypes.bfloat16)
    return (high, low)


def angles(rows, cols, length):
    grid = np.outer(np.arange(rows), np.arange(cols)) % length
    return grid * (2.0 * math.pi / length)


def blocked_pair(angle, width):
    rows, cols = angle.shape
    cosine = np.cos(angle).reshape(rows, cols // width, width)
    sine = np.sin(angle).reshape(rows, cols // width, width)
    return np.concatenate([cosine, sine], axis=2).transpose(1, 0, 2)


def split(value):
    high = value.astype(jnp.bfloat16)
    return (high, (value - high.astype(jnp.float32)).astype(jnp.bfloat16))


def product(left_high, left_low, right_high, right_low):
    def dot(a, b):
        return jnp.dot(a, b, preferred_element_type=jnp.float32)

    return dot(left_high, right_high) + (dot(left_high, right_low) + dot(left_low, right_high))


def greet(tx, ty, ntx, nty):
    barrier = pltpu.get_barrier_semaphore()
    for step in range(1, ntx):
        pl.semaphore_signal(
            barrier, inc=1, device_id=(lax.rem(tx + step, ntx), ty), device_id_type=MESH
        )
    for step in range(1, nty):
        pl.semaphore_signal(
            barrier, inc=1, device_id=(tx, lax.rem(ty + step, nty)), device_id_type=MESH
        )
    pl.semaphore_wait(barrier, ntx + nty - 2)


def send_over(axis, step, part, source, target, sems, ntx, nty):
    tx, ty = lax.axis_index("tx"), lax.axis_index("ty")
    if axis == "tx":
        dest = lax.rem(tx + step, ntx)
        mine, device = tx, (dest, ty)
    else:
        dest = lax.rem(ty + step, nty)
        mine, device = ty, (tx, dest)
    return pltpu.make_async_remote_copy(
        src_ref=source.at[dest, part],
        dst_ref=target.at[mine, part],
        send_sem=sems[0].at[part, step],
        recv_sem=sems[1].at[part, step],
        device_id=device,
        device_id_type=MESH,
    )


def conductivity(absolute, multiplier, nodes):
    count = nodes.shape[0]
    spacing = TABLE_SPAN / (count - 1)
    total = jnp.zeros_like(absolute) + nodes[0]
    for index in range(count - 1):
        place = (absolute - (TABLE_LOW + index * spacing)) * (1.0 / spacing)
        total = total + (nodes[index + 1] - nodes[index]) * jnp.clip(place, 0.0, 1.0)
    return multiplier * total


def of_kind(kind, values):
    result = jnp.zeros(kind.shape, jnp.float32)
    for grain in range(values.shape[0]):
        result = result + jnp.where(kind == grain, values[grain], 0.0)
    return result


def laser_plane(rows, width, tx, ty, ntx, row_spot, col_spot):
    total = ntx * width
    row_ids = lax.broadcasted_iota(jnp.int32, (rows, width), 0) + ty * rows
    col_ids = lax.broadcasted_iota(jnp.int32, (rows, width), 1) + tx * width
    along = col_ids - col_spot + total // 2
    along = jnp.where(along < 0, along + total, along)
    along = jnp.where(along >= total, along - total, along) - total // 2
    along = along.astype(jnp.float32) * (1.0 / (0.5 * width))
    across = (row_ids - row_spot).astype(jnp.float32) * (1.0 / rows)
    return jnp.exp(-0.5 * across * across) * jnp.exp(-0.5 * along * along)


def heat_sweeps(
    ntx, nty, heat, kind, nodes, factor, row_spots, col_spots, rows_out, rows_in, cols_out, cols_in,
    edge_send, edge_recv,
):
    tx, ty = lax.axis_index("tx"), lax.axis_index("ty")
    sheets, rows, width = heat.shape
    flat, cube = (sheets * rows, width), (sheets, rows, width)
    lane = lax.broadcasted_iota(jnp.int32, cube, 2)
    line = lax.broadcasted_iota(jnp.int32, cube, 1)
    theta = heat[...] - AMBIENT_HEAT
    multiplier = of_kind(kind[...], factor)
    started = []
    for sweep in range(SWEEPS):
        cond = conductivity(theta + AMBIENT_HEAT, multiplier, nodes)
        pair = (theta, cond)
        for place, value in enumerate(pair):
            rows_out[sweep, 0, place] = value[:, 0, :]
            rows_out[sweep, 1, place] = value[:, rows - 1, :]
            turned = value.reshape(flat).T
            cols_out[sweep, 0, place : place + 1] = turned[:1]
            cols_out[sweep, 1, place : place + 1] = turned[width - 1 :]
        copies = []
        for side, shift in enumerate((-1, 1)):
            targets = (
                (cols_out, cols_in, (lax.rem(tx + shift + ntx, ntx), ty)),
                (rows_out, rows_in, (tx, lax.rem(ty + shift + nty, nty))),
            )
            for axis, (source, target, device) in enumerate(targets):
                copy = pltpu.make_async_remote_copy(
                    src_ref=source.at[sweep, side],
                    dst_ref=target.at[sweep, side],
                    send_sem=edge_send.at[sweep, side, axis],
                    recv_sem=edge_recv.at[sweep, side, axis],
                    device_id=device,
                    device_id_type=MESH,
                )
                copy.start()
                copies.append(copy)
        started += copies
        plane = laser_plane(rows, width, tx, ty, ntx, row_spots[sweep], col_spots[sweep])
        heating = jnp.stack([plane * math.exp(-sheet / LASER_DEPTH) for sheet in range(sheets)])
        vertical = 0.5 * (cond[1:] + cond[:-1]) * (theta[1:] - theta[:-1])
        zero_layer = jnp.zeros_like(theta[:1])
        flux = jnp.concatenate([vertical, zero_layer], 0) - jnp.concatenate(
            [zero_layer, vertical], 0
        )
        for copy in copies:
            copy.wait_recv()
        for side, shift in enumerate((-1, 1)):
            turned = cols_in[sweep, side].T
            edge = 0 if shift == 1 else width - 1
            other = []
            for place, value in enumerate(pair):
                moved = pltpu.roll(value.reshape(flat), shift % width, 1).reshape(cube)
                column = turned[:, place : place + 1].reshape(sheets, rows, 1)
                other.append(jnp.where(lane == edge, column, moved))
            flux = flux + 0.5 * (cond + other[1]) * (other[0] - theta)
            edge = 0 if shift == 1 else rows - 1
            inside = ty > 0 if shift == 1 else ty < nty - 1
            other = []
            for place, value in enumerate(pair):
                moved = pltpu.roll(value.reshape(flat), shift % flat[0], 0).reshape(cube)
                row = jnp.where(inside, rows_in[sweep, side, place], 0.0)
                other.append(jnp.where(line == edge, row[:, None, :], moved))
            flux = flux + 0.5 * (cond + other[1]) * (other[0] - theta)
        theta = theta + STEP_RATE * (flux + LASER_POWER * heating)
    return theta + AMBIENT_HEAT, started


def edge_scratch(sheets, rows, width):
    edge_rows = pltpu.VMEM((SWEEPS, 2, 2, sheets, width), jnp.float32)
    edge_cols = pltpu.VMEM((SWEEPS, 2, 8, sheets * rows), jnp.float32)
    sems = pltpu.SemaphoreType.DMA((SWEEPS, 2, 2))
    return [edge_rows, edge_rows, edge_cols, edge_cols, sems, sems]


def forward_kernel(
    ntx, nty, heat, kind, moment, nodes, factor, threshold, row_spots, col_spots, table_high,
    table_low, warmed, out, proportion, layered, gathered, left_high, left_low, blocks, rows_out,
    rows_in, cols_out, cols_in, edge_send, edge_recv, tx_send, tx_recv, ty_send, ty_recv,
):
    tx, ty = lax.axis_index("tx"), lax.axis_index("ty")
    parts, sheets, rows, width = moment.shape
    greet(tx, ty, ntx, nty)
    cols_out[...] = jnp.zeros_like(cols_out)
    state, edges = heat_sweeps(
        ntx, nty, heat, kind, nodes, factor, row_spots, col_spots, rows_out, rows_in, cols_out,
        cols_in, edge_send, edge_recv,
    )
    warmed[...] = state
    proportion[...] = jax.nn.sigmoid(
        (of_kind(kind[...], threshold) - state) * (1.0 / ORDERING_SPREAD)
    )
    count = 2 * sheets
    own = count // ntx
    tx_sems, ty_sems = (tx_send, tx_recv), (ty_send, ty_recv)

    def over_tx(step, part):
        return send_over("tx", step, part, layered, gathered, tx_sems, ntx, nty)

    def over_ty(step, part):
        return send_over("ty", step, part, blocks, out, ty_sems, ntx, nty)

    def layer_part(part, carry):
        for freq in range(sheets + 1):
            real = jnp.zeros((rows, width), jnp.float32)
            imag = jnp.zeros((rows, width), jnp.float32)
            for sheet in range(sheets):
                value = moment[part, sheet] * proportion[sheet]
                angle = 2.0 * math.pi * (sheet * freq % count) / count
                real = real + value * math.cos(angle)
                imag = imag - value * math.sin(angle)
            layered[freq // own, part, 0, freq % own] = real
            layered[freq // own, part, 1, freq % own] = imag
            if 0 < freq < sheets:
                other = count - freq
                layered[other // own, part, 0, other % own] = real
                layered[other // own, part, 1, other % own] = -imag
        return carry

    for part in range(parts):
        layer_part(part, 0)
        for step in range(1, ntx):
            over_tx(step, part).start()

    def transform(block, part):
        result = product(left_high[...], left_low[...], table_high[block], table_low[block])
        half = own * rows
        real = result[:half, :width] + result[half:, width:]
        imag = result[half:, :width] - result[:half, width:]
        return real.reshape(own, rows, width), imag.reshape(own, rows, width)

    def transform_part(part, carry):
        for step in range(1, ntx):
            over_tx(step, part).wait_recv()
        gathered[tx, part] = layered[tx, part]
        for source in range(ntx):
            high, low = split(gathered[source, part].reshape(2 * own * rows, width))
            left_high[:, source * width : (source + 1) * width] = high
            left_low[:, source * width : (source + 1) * width] = low

        def one(step, inner):
            block = lax.rem(ty + step, nty)
            real, imag = transform(block, part)
            blocks[block, part, :, :, :width] = real
            blocks[block, part, :, :, width:] = imag
            over_ty(step, part).start()
            return inner

        lax.fori_loop(1, nty, one, 0)
        real, imag = transform(ty, part)
        out[ty, part, :, :, :width] = real
        out[ty, part, :, :, width:] = imag
        return carry

    lax.fori_loop(0, parts, transform_part, 0)
    for edge in edges:
        edge.wait_send()
    for part in range(parts):
        for step in range(1, ntx):
            over_tx(step, part).wait_send()
        for step in range(1, nty):
            over_ty(step, part).wait()


def backward_kernel(
    ntx, nty, arrived, tensor_hbm, fwd_high, fwd_low, back_high, back_low, x_high_hbm, x_low_hbm,
    layers, out, tensor, x_high, x_low, spectra, field, returned, left_high, left_low, partial,
    landed, local_sem, ty_send, ty_recv, tx_send, tx_recv,
):
    tx, ty = lax.axis_index("tx"), lax.axis_index("ty")
    parts, own, rows = arrived.shape[1:4]
    width = arrived.shape[4] // 2
    total = nty * rows
    sheets = out.shape[1]
    tx_sems, ty_sems = (tx_send, tx_recv), (ty_send, ty_recv)
    loads = [
        pltpu.make_async_copy(tensor_hbm, tensor, local_sem.at[0]),
        pltpu.make_async_copy(x_high_hbm, x_high, local_sem.at[1]),
        pltpu.make_async_copy(x_low_hbm, x_low, local_sem.at[2]),
    ]
    for load in loads:
        load.start()

    def over_ty(step, part):
        return send_over("ty", step, part, field, returned, ty_sems, ntx, nty)

    def over_tx(step, part):
        return send_over("tx", step, part, partial, landed, tx_sems, ntx, nty)

    def forward_rows(index, carry):
        part, freq = index // own, index % own
        high, low = split(arrived[:, part, freq].reshape(total, 2 * width))
        result = product(fwd_high[...], fwd_low[...], high, low)
        half = 2 * total
        spectra[part, freq, :, :width] = result[:half, :width] + result[half:, width:]
        spectra[part, freq, :, width:] = result[:half, width:] - result[half:, :width]
        return carry

    lax.fori_loop(0, parts * own, forward_rows, 0)
    greet(tx, ty, ntx, nty)
    loads[0].wait()
    for part in range(parts):

        def back_rows(freq, carry):
            sides = []
            for side in range(2):
                lanes = slice(side * width, (side + 1) * width)
                sides.append(
                    tensor[PAIRS[part][0], freq] * spectra[0, freq, :, lanes]
                    + tensor[PAIRS[part][1], freq] * spectra[1, freq, :, lanes]
                    + tensor[PAIRS[part][2], freq] * spectra[2, freq, :, lanes]
                )
            high, low = split(jnp.concatenate(sides, axis=1))
            result = product(back_high[...], back_low[...], high, low)
            real = result[:total, :width] - result[total:, width:]
            imag = result[:total, width:] + result[total:, :width]
            field[:, part, 0, freq] = real.reshape(nty, rows, width)
            field[:, part, 1, freq] = imag.reshape(nty, rows, width)
            return carry

        lax.fori_loop(0, own, back_rows, 0)
        for step in range(1, nty):
            over_ty(step, part).start()
        returned[ty, part] = field[ty, part]
    loads[1].wait()
    loads[2].wait()

    def transform(block):
        result = product(left_high[...], left_low[...], x_high[block], x_low[block])
        half = own * rows
        real = result[:half, :width] - result[half:, width:]
        imag = result[:half, width:] + result[half:, :width]
        real, imag = real.reshape(own, rows, width), imag.reshape(own, rows, width)
        values = []
        for sheet in range(sheets):
            value = jnp.zeros((rows, width), jnp.float32)
            for freq in range(own):
                value = value + layers[tx * own + freq, 2 * sheet] * real[freq]
                value = value - layers[tx * own + freq, 2 * sheet + 1] * imag[freq]
            values.append(value)
        return values

    def inverse_part(part, carry):
        for step in range(1, nty):
            over_ty(step, part).wait_recv()
        for source in range(nty):
            high, low = split(returned[source, part].reshape(2 * own * rows, width))
            left_high[:, source * width : (source + 1) * width] = high
            left_low[:, source * width : (source + 1) * width] = low

        def one(step, inner):
            block = lax.rem(tx + step, ntx)
            for sheet, value in enumerate(transform(block)):
                partial[block, part, sheet] = value
            over_tx(step, part).start()
            return inner

        lax.fori_loop(1, ntx, one, 0)
        for sheet, value in enumerate(transform(tx)):
            landed[tx, part, sheet] = value
        return carry

    lax.fori_loop(0, parts, inverse_part, 0)
    for part in range(parts):
        for step in range(1, ntx):
            over_tx(step, part).wait_recv()
        total_field = landed[0, part]
        for source in range(1, ntx):
            total_field = total_field + landed[source, part]
        out[part] = total_field
    for part in range(parts):
        for step in range(1, nty):
            over_ty(step, part).wait_send()
        for step in range(1, ntx):
            over_tx(step, part).wait_send()


def vmem():
    return pl.BlockSpec(memory_space=pltpu.VMEM)


def params(identity):
    return pltpu.CompilerParams(
        collective_id=identity, has_side_effects=True, vmem_limit_bytes=60 * 1024 * 1024
    )


def spectra_over_rows(heat, kind, moment, scalars, ntx, nty):
    parts, sheets, rows, width = moment.shape
    own = 2 * sheets // ntx
    high, low = halves(blocked_pair(angles(ntx * width, nty * width, 2 * ntx * width), width))
    lines = 2 * own * rows
    dma = pltpu.SemaphoreType.DMA
    return pl.pallas_call(
        functools.partial(forward_kernel, ntx, nty),
        out_shape=(
            jax.ShapeDtypeStruct(heat.shape, jnp.float32),
            jax.ShapeDtypeStruct((nty, parts, own, rows, 2 * width), jnp.float32),
        ),
        in_specs=[vmem()] * 3
        + [pl.BlockSpec(memory_space=pltpu.SMEM)] * len(scalars)
        + [vmem()] * 2,
        out_specs=(vmem(), vmem()),
        scratch_shapes=[
            pltpu.VMEM((sheets, rows, width), jnp.float32),
            pltpu.VMEM((ntx, parts, 2, own, rows, width), jnp.float32),
            pltpu.VMEM((ntx, parts, 2, own, rows, width), jnp.float32),
            pltpu.VMEM((lines, ntx * width), jnp.bfloat16),
            pltpu.VMEM((lines, ntx * width), jnp.bfloat16),
            pltpu.VMEM((nty, parts, own, rows, 2 * width), jnp.float32),
            *edge_scratch(sheets, rows, width),
            dma((parts, ntx)),
            dma((parts, ntx)),
            dma((parts, nty)),
            dma((parts, nty)),
        ],
        compiler_params=params(0),
        name="forward_spectra",
    )(heat, kind, moment, *scalars, high, low)


def field_from_spectra(arrived, stray_tensor, sheets, ntx, nty):
    parts, own, rows = arrived.shape[1:4]
    width = arrived.shape[4] // 2
    total, columns = nty * rows, ntx * width
    count = 2 * sheets
    forward = angles(2 * total, total, 2 * total)
    forward = halves(np.concatenate([np.cos(forward), np.sin(forward)], axis=0))
    back = angles(total, 2 * total, 2 * total)
    back = halves(np.concatenate([np.cos(back), np.sin(back)], axis=0))
    x_table = halves(blocked_pair(angles(nty * width, columns, 2 * columns), width))
    turn = angles(count, sheets, count)
    scale = -1.0 / (count * 2 * total * 2 * columns)
    layers = np.stack([np.cos(turn), np.sin(turn)], axis=2).reshape(count, 2 * sheets) * scale
    lines = 2 * own * rows
    dma = pltpu.SemaphoreType.DMA
    anywhere = pl.BlockSpec(memory_space=pl.ANY)
    return pl.pallas_call(
        functools.partial(backward_kernel, ntx, nty),
        out_shape=jax.ShapeDtypeStruct((parts, sheets, rows, width), jnp.float32),
        in_specs=[vmem(), anywhere, vmem(), vmem(), vmem(), vmem(), anywhere, anywhere]
        + [pl.BlockSpec(memory_space=pltpu.SMEM)],
        out_specs=vmem(),
        scratch_shapes=[
            pltpu.VMEM(stray_tensor.shape, jnp.float32),
            pltpu.VMEM(x_table[0].shape, jnp.bfloat16),
            pltpu.VMEM(x_table[1].shape, jnp.bfloat16),
            pltpu.VMEM((parts, own, 2 * total, 2 * width), jnp.float32),
            pltpu.VMEM((nty, parts, 2, own, rows, width), jnp.float32),
            pltpu.VMEM((nty, parts, 2, own, rows, width), jnp.float32),
            pltpu.VMEM((lines, nty * width), jnp.bfloat16),
            pltpu.VMEM((lines, nty * width), jnp.bfloat16),
            pltpu.VMEM((ntx, parts, sheets, rows, width), jnp.float32),
            pltpu.VMEM((ntx, parts, sheets, rows, width), jnp.float32),
            dma((3,)),
            dma((parts, nty)),
            dma((parts, nty)),
            dma((parts, ntx)),
            dma((parts, ntx)),
        ],
        compiler_params=params(1),
        name="field_return",
    )(arrived, stray_tensor, *forward, *back, *x_table, layers.astype(np.float32))


def deep_table(table, axis):
    high, low = halves(table)
    return np.concatenate([high, low, high], axis=axis)


def deep_dot(table, high, low):
    data = jnp.concatenate([high, high, low], axis=0)
    return jnp.dot(table[...], data, preferred_element_type=jnp.float32)


def row_units(own, rows, cut):
    units = []
    for freq in range(own):
        pieces = 2 if freq == cut else 1
        lines = rows // pieces
        units += [(freq, piece * lines, lines) for piece in range(pieces)]
    return units


def send_rows(axis, step, unit, units, source, target, sems, ntx, nty):
    tx, ty = lax.axis_index("tx"), lax.axis_index("ty")
    freq, first, lines = units[unit]
    if axis == "tx":
        dest = lax.rem(tx + step, ntx)
        mine, device = tx, (dest, ty)
    else:
        dest = lax.rem(ty + step, nty)
        mine, device = ty, (tx, dest)
    span = (slice(None),) * (len(source.shape) - 4) + (pl.ds(first, lines),)
    return pltpu.make_async_remote_copy(
        src_ref=source.at[(dest, freq) + span],
        dst_ref=target.at[(mine, freq) + span],
        send_sem=sems[0].at[unit, step],
        recv_sem=sems[1].at[unit, step],
        device_id=device,
        device_id_type=MESH,
    )


def settle(*values):
    def kernel(*refs):
        count = len(values)
        sems = refs[-1]
        copies = [
            pltpu.make_async_copy(refs[index], refs[count + index], sems.at[index])
            for index in range(count)
        ]
        for copy in copies:
            copy.start()
        for copy in copies:
            copy.wait()

    anywhere = pl.BlockSpec(memory_space=pl.ANY)
    return pl.pallas_call(
        kernel,
        out_shape=tuple(jax.ShapeDtypeStruct(value.shape, value.dtype) for value in values),
        in_specs=[anywhere] * len(values),
        out_specs=(anywhere,) * len(values),
        scratch_shapes=[pltpu.SemaphoreType.DMA((len(values),))],
        name="settle",
    )(*values)


def whole_kernel(
    ntx, nty, heat, kind, nodes, factor, threshold, row_spots, col_spots, moment_hbm, to_hbm,
    forward_hbm, tensor_hbm, back_hbm, from_hbm, warmed, out, proportion, layered, gathered,
    blocks, arrived, spectra, field, returned, partial, landed, moment, to_table, forward_table,
    tensor, back_table, from_table, along_input, inverse_input, rows_out, rows_in, cols_out,
    cols_in, edge_send, edge_recv, local_sem, tx_send, tx_recv, ty_send, ty_recv, ty_back_send,
    ty_back_recv, tx_back_send, tx_back_recv,
):
    tx, ty = lax.axis_index("tx"), lax.axis_index("ty")
    parts, sheets, rows, width = moment.shape
    count = 2 * sheets
    own = count // ntx
    total = nty * rows
    ahead, behind = row_units(own, rows, 0), row_units(own, rows, own - 1)
    loads = [
        pltpu.make_async_copy(source, target, local_sem.at[index])
        for index, (source, target) in enumerate(
            (
                (moment_hbm, moment),
                (to_hbm, to_table),
                (forward_hbm, forward_table),
                (tensor_hbm, tensor),
                (back_hbm, back_table),
                (from_hbm, from_table),
            )
        )
    ]
    for load in loads:
        load.start()

    def tx_copy(step, unit):
        sems = (tx_send, tx_recv)
        return send_rows("tx", step, unit, ahead, layered, gathered, sems, ntx, nty)

    def ty_copy(step, unit):
        sems = (ty_send, ty_recv)
        return send_rows("ty", step, unit, ahead, blocks, arrived, sems, ntx, nty)

    def ty_return(step, unit):
        sems = (ty_back_send, ty_back_recv)
        return send_rows("ty", step, unit, behind, field, returned, sems, ntx, nty)

    def tx_return(step, unit):
        sems = (tx_back_send, tx_back_recv)
        return send_rows("tx", step, unit, behind, partial, landed, sems, ntx, nty)

    def start_all(copy, size, unit):
        for step in range(1, size):
            copy(step, unit).start()

    def await_all(copy, size, unit):
        for step in range(1, size):
            copy(step, unit).wait_recv()

    greet(tx, ty, ntx, nty)
    cols_out[...] = jnp.zeros_like(cols_out)
    state, edges = heat_sweeps(
        ntx, nty, heat, kind, nodes, factor, row_spots, col_spots, rows_out, rows_in, cols_out,
        cols_in, edge_send, edge_recv,
    )
    warmed[...] = state
    proportion[...] = jax.nn.sigmoid(
        (of_kind(kind[...], threshold) - state) * (1.0 / ORDERING_SPREAD)
    )

    def layer_spectra(freqs):
        def layer_part(part, carry):
            values = [moment[part, sheet] * proportion[sheet] for sheet in range(sheets)]
            for freq in freqs:
                real = jnp.zeros((rows, width), jnp.float32)
                imag = jnp.zeros((rows, width), jnp.float32)
                for sheet in range(sheets):
                    angle = 2.0 * math.pi * (sheet * freq % count) / count
                    real = real + values[sheet] * math.cos(angle)
                    imag = imag - values[sheet] * math.sin(angle)
                layered[freq // own, freq % own, 0, part] = real
                layered[freq // own, freq % own, 1, part] = imag
                if 0 < freq < sheets:
                    other = count - freq
                    layered[other // own, other % own, 0, part] = real
                    layered[other // own, other % own, 1, part] = -imag
            return carry

        lax.fori_loop(0, parts, layer_part, 0)

    loads[0].wait()
    ready = set()
    for freq in range(own):
        needed = []
        for line in range(sheets + 1):
            if line not in ready and freq in (line % own, (count - line) % own):
                needed.append(line)
        if needed:
            layer_spectra(needed)
            ready.update(needed)
        for unit in range(AHEAD):
            if ahead[unit][0] == freq:
                start_all(tx_copy, ntx, unit)

    def assemble(source, piece, size, target):
        freq, first, lines = piece
        depth = size * width
        for index in range(size):
            value = source[index, freq, :, :, first : first + lines]
            high, low = split(value.reshape(2 * parts * lines, width))
            for place, half in enumerate((high, high, low)):
                start = place * depth + index * width
                target[: 2 * parts * lines, start : start + width] = half

    def multiply(source, table, lines, sign):
        half = parts * lines
        result = jnp.dot(source[: 2 * half], table, preferred_element_type=jnp.float32)
        real = result[:half, :width] + sign * result[half:, width:]
        imag = result[half:, :width] - sign * result[:half, width:]
        return real.reshape(parts, lines, width), imag.reshape(parts, lines, width)

    def forward_columns(unit):
        freq, first, lines = ahead[unit]
        span = slice(first, first + lines)
        await_all(tx_copy, ntx, unit)
        if unit + AHEAD < len(ahead):
            start_all(tx_copy, ntx, unit + AHEAD)
        gathered[tx, freq, :, :, span] = layered[tx, freq, :, :, span]
        assemble(gathered, ahead[unit], ntx, along_input)
        if unit == 0:
            loads[1].wait()

        def one(step, carry):
            block = lax.rem(ty + step, nty)
            real, imag = multiply(along_input, to_table[block], lines, 1.0)
            blocks[block, freq, :, span, :width] = real
            blocks[block, freq, :, span, width:] = imag
            ty_copy(step, unit).start()
            return carry

        lax.fori_loop(1, nty, one, 0)
        real, imag = multiply(along_input, to_table[ty], lines, 1.0)
        arrived[ty, freq, :, span, :width] = real
        arrived[ty, freq, :, span, width:] = imag

    def through_rows(freq):
        for unit, piece in enumerate(ahead):
            if piece[0] == freq:
                await_all(ty_copy, nty, unit)
        if freq == 0:
            for load in loads[2:5]:
                load.wait()

        def forward_rows(part, carry):
            high, low = split(arrived[:, freq, part].reshape(total, 2 * width))
            result = deep_dot(forward_table, high, low)
            top = 2 * total
            spectra[part, :, :width] = result[:top, :width] + result[top:, width:]
            spectra[part, :, width:] = result[:top, width:] - result[top:, :width]
            return carry

        lax.fori_loop(0, parts, forward_rows, 0)
        for part in range(parts):
            sides = []
            for side in range(2):
                lanes = slice(side * width, (side + 1) * width)
                sides.append(
                    tensor[PAIRS[part][0], freq] * spectra[0, :, lanes]
                    + tensor[PAIRS[part][1], freq] * spectra[1, :, lanes]
                    + tensor[PAIRS[part][2], freq] * spectra[2, :, lanes]
                )
            high, low = split(jnp.concatenate(sides, axis=1))
            result = deep_dot(back_table, high, low)
            real = result[:total, :width] - result[total:, width:]
            imag = result[:total, width:] + result[total:, :width]
            field[:, freq, 0, part] = real.reshape(nty, rows, width)
            field[:, freq, 1, part] = imag.reshape(nty, rows, width)
        for unit, piece in enumerate(behind):
            if piece[0] == freq:
                start_all(ty_return, nty, unit)
        returned[ty, freq] = field[ty, freq]

    def inverse_columns(unit):
        freq, first, lines = behind[unit]
        span = slice(first, first + lines)
        await_all(ty_return, nty, unit)
        assemble(returned, behind[unit], nty, inverse_input)
        if unit == 0:
            loads[5].wait()

        def one(step, carry):
            block = lax.rem(tx + step, ntx)
            real, imag = multiply(inverse_input, from_table[block], lines, -1.0)
            partial[block, freq, 0, :, span] = real
            partial[block, freq, 1, :, span] = imag
            tx_return(step, unit).start()
            return carry

        lax.fori_loop(1, ntx, one, 0)
        real, imag = multiply(inverse_input, from_table[tx], lines, -1.0)
        landed[tx, freq, 0, :, span] = real
        landed[tx, freq, 1, :, span] = imag

    for turn in range(own + 3):
        for unit, piece in enumerate(ahead):
            if piece[0] == turn:
                forward_columns(unit)
        if 0 <= turn - 1 < own:
            through_rows(turn - 1)
        for unit, piece in enumerate(behind):
            if piece[0] == turn - 3:
                inverse_columns(unit)

    scale = -1.0 / (count * 2 * total * 2 * ntx * width)
    for unit, (freq, first, lines) in enumerate(behind):
        span = slice(first, first + lines)
        await_all(tx_return, ntx, unit)

        def back_layers(part, carry):
            for sheet in range(sheets):
                value = jnp.zeros((lines, width), jnp.float32)
                if freq > 0:
                    value = out[part, sheet, span]
                for source in range(ntx):
                    line = source * own + freq
                    angle = 2.0 * math.pi * (sheet * line % count) / count
                    value = value + landed[source, freq, 0, part, span] * (scale * math.cos(angle))
                    value = value - landed[source, freq, 1, part, span] * (scale * math.sin(angle))
                out[part, sheet, span] = value
            return carry

        lax.fori_loop(0, parts, back_layers, 0)

    for edge in edges:
        edge.wait_send()
    for unit in range(len(ahead)):
        for copy, size in ((tx_copy, ntx), (ty_copy, nty), (ty_return, nty), (tx_return, ntx)):
            for step in range(1, size):
                copy(step, unit).wait_send()


def everything(heat, kind, moment, stray_tensor, scalars, ntx, nty):
    parts, sheets, rows, width = moment.shape
    own = 2 * sheets // ntx
    total, columns = nty * rows, ntx * width
    forward = angles(2 * total, total, 2 * total)
    forward = deep_table(np.concatenate([np.cos(forward), np.sin(forward)], axis=0), 1)
    back = angles(total, 2 * total, 2 * total)
    back = deep_table(np.concatenate([np.cos(back), np.sin(back)], axis=0), 1)
    to_table = deep_table(blocked_pair(angles(columns, nty * width, 2 * columns), width), 1)
    from_table = deep_table(blocked_pair(angles(nty * width, columns, 2 * columns), width), 1)
    lines = 2 * parts * rows
    dma = pltpu.SemaphoreType.DMA
    anywhere = pl.BlockSpec(memory_space=pl.ANY)
    over_tx = pltpu.VMEM((ntx, own, 2, parts, rows, width), jnp.float32)
    over_ty = pltpu.VMEM((nty, own, parts, rows, 2 * width), jnp.float32)
    back_ty = pltpu.VMEM((nty, own, 2, parts, rows, width), jnp.float32)
    units = len(row_units(own, rows, 0))
    return settle(*pl.pallas_call(
        functools.partial(whole_kernel, ntx, nty),
        out_shape=(
            jax.ShapeDtypeStruct(heat.shape, jnp.float32),
            jax.ShapeDtypeStruct(moment.shape, jnp.float32),
        ),
        in_specs=[vmem()] * 2
        + [pl.BlockSpec(memory_space=pltpu.SMEM)] * len(scalars)
        + [anywhere] * 6,
        out_specs=(vmem(), vmem()),
        scratch_shapes=[
            pltpu.VMEM((sheets, rows, width), jnp.float32),
            over_tx,
            over_tx,
            over_ty,
            over_ty,
            pltpu.VMEM((parts, 2 * total, 2 * width), jnp.float32),
            back_ty,
            back_ty,
            over_tx,
            over_tx,
            pltpu.VMEM(moment.shape, jnp.float32),
            pltpu.VMEM(to_table.shape, jnp.bfloat16),
            pltpu.VMEM(forward.shape, jnp.bfloat16),
            pltpu.VMEM(stray_tensor.shape, jnp.float32),
            pltpu.VMEM(back.shape, jnp.bfloat16),
            pltpu.VMEM(from_table.shape, jnp.bfloat16),
            pltpu.VMEM((lines, 3 * columns), jnp.bfloat16),
            pltpu.VMEM((lines, 3 * nty * width), jnp.bfloat16),
            *edge_scratch(sheets, rows, width),
            dma((6,)),
            dma((units, ntx)),
            dma((units, ntx)),
            dma((units, nty)),
            dma((units, nty)),
            dma((units, nty)),
            dma((units, nty)),
            dma((units, ntx)),
            dma((units, ntx)),
        ],
        compiler_params=params(2),
        name="demagnetize",
    )(heat, kind, *scalars, moment, to_table, forward, stray_tensor, back, from_table))


def local(
    reduced_heat,
    substance_kind,
    moment_vector,
    stray_tensor,
    diffusivity_nodes,
    substance_factor,
    ordering_threshold,
    beam_transverse_spot,
    beam_downtrack_spot,
):
    ntx, nty = lax.axis_size("tx"), lax.axis_size("ty")
    scalars = (
        diffusivity_nodes,
        substance_factor,
        ordering_threshold,
        beam_transverse_spot,
        beam_downtrack_spot,
    )
    if 16 * ntx * nty * reduced_heat.shape[2] ** 2 <= TABLE_BYTES:
        return everything(
            reduced_heat, substance_kind, moment_vector, stray_tensor, scalars, ntx, nty
        )
    warmed_state, arrived = spectra_over_rows(
        reduced_heat, substance_kind, moment_vector, scalars, ntx, nty
    )
    demag_field = field_from_spectra(arrived, stray_tensor, reduced_heat.shape[0], ntx, nty)
    return (warmed_state, demag_field)


def solution(mesh):
    in_specs = (
        P(None, "ty", "tx"),
        P(None, "ty", "tx"),
        P(None, None, "ty", "tx"),
        P(None, "tx", None, "ty"),
        P(),
        P(),
        P(),
        P(),
        P(),
    )
    out_specs = (P(None, "ty", "tx"), P(None, None, "ty", "tx"))
    return jax.shard_map(local, mesh=mesh, in_specs=in_specs, out_specs=out_specs, check_vma=False)
```

```python
import functools
import math

import jax
import jax.numpy as jnp
import ml_dtypes
import numpy as np
from jax import lax
from jax.experimental import pallas as pl
from jax.experimental.pallas import tpu as pltpu
from jax.sharding import PartitionSpec as P

SWEEPS = 2


AMBIENT_HEAT = 0.3
STEP_RATE = 0.05
LASER_POWER = 4.0
LASER_DEPTH = 4.0
ORDERING_SPREAD = 0.08
TABLE_LOW = 0.2
TABLE_SPAN = 1.6


MESH = pl.DeviceIdType.MESH
AHEAD = 2
TABLE_BYTES = 16 * 1024 * 1024
PAIRS = ((0, 3, 4), (3, 1, 5), (4, 5, 2))


def halves(table):
    high = table.astype(ml_dtypes.bfloat16)
    low = (table - high.astype(np.float64)).astype(ml_dtypes.bfloat16)
    return (high, low)


def angles(rows, cols, length):
    grid = np.outer(np.arange(rows), np.arange(cols)) % length
    return grid * (2.0 * math.pi / length)


def blocked_pair(angle, width):
    rows, cols = angle.shape
    cosine = np.cos(angle).reshape(rows, cols // width, width)
    sine = np.sin(angle).reshape(rows, cols // width, width)
    return np.concatenate([cosine, sine], axis=2).transpose(1, 0, 2)


def split(value):
    high = value.astype(jnp.bfloat16)
    return (high, (value - high.astype(jnp.float32)).astype(jnp.bfloat16))


def product(left_high, left_low, right_high, right_low):
    def dot(a, b):
        return jnp.dot(a, b, preferred_element_type=jnp.float32)

    return dot(left_high, right_high) + (dot(left_high, right_low) + dot(left_low, right_high))


def greet(tx, ty, ntx, nty):
    barrier = pltpu.get_barrier_semaphore()
    for step in range(1, ntx):
        pl.semaphore_signal(
            barrier, inc=1, device_id=(lax.rem(tx + step, ntx), ty), device_id_type=MESH
        )
    for step in range(1, nty):
        pl.semaphore_signal(
            barrier, inc=1, device_id=(tx, lax.rem(ty + step, nty)), device_id_type=MESH
        )
    pl.semaphore_wait(barrier, ntx + nty - 2)


def send_over(axis, step, part, source, target, sems, ntx, nty):
    tx, ty = lax.axis_index("tx"), lax.axis_index("ty")
    if axis == "tx":
        dest = lax.rem(tx + step, ntx)
        mine, device = tx, (dest, ty)
    else:
        dest = lax.rem(ty + step, nty)
        mine, device = ty, (tx, dest)
    return pltpu.make_async_remote_copy(
        src_ref=source.at[dest, part],
        dst_ref=target.at[mine, part],
        send_sem=sems[0].at[part, step],
        recv_sem=sems[1].at[part, step],
        device_id=device,
        device_id_type=MESH,
    )


def conductivity(absolute, multiplier, nodes):
    count = nodes.shape[0]
    spacing = TABLE_SPAN / (count - 1)
    total = jnp.zeros_like(absolute) + nodes[0]
    for index in range(count - 1):
        place = (absolute - (TABLE_LOW + index * spacing)) * (1.0 / spacing)
        total = total + (nodes[index + 1] - nodes[index]) * jnp.clip(place, 0.0, 1.0)
    return multiplier * total


def of_kind(kind, values):
    result = jnp.zeros(kind.shape, jnp.float32)
    for grain in range(values.shape[0]):
        result = result + jnp.where(kind == grain, values[grain], 0.0)
    return result


def laser_plane(rows, width, tx, ty, ntx, row_spot, col_spot):
    total = ntx * width
    row_ids = lax.broadcasted_iota(jnp.int32, (rows, width), 0) + ty * rows
    col_ids = lax.broadcasted_iota(jnp.int32, (rows, width), 1) + tx * width
    along = col_ids - col_spot + total // 2
    along = jnp.where(along < 0, along + total, along)
    along = jnp.where(along >= total, along - total, along) - total // 2
    along = along.astype(jnp.float32) * (1.0 / (0.5 * width))
    across = (row_ids - row_spot).astype(jnp.float32) * (1.0 / rows)
    return jnp.exp(-0.5 * across * across) * jnp.exp(-0.5 * along * along)


def heat_sweeps(
    ntx, nty, heat, kind, nodes, factor, row_spots, col_spots, rows_out, rows_in, cols_out, cols_in,
    edge_send, edge_recv,
):
    tx, ty = lax.axis_index("tx"), lax.axis_index("ty")
    sheets, rows, width = heat.shape
    flat, cube = (sheets * rows, width), (sheets, rows, width)
    lane = lax.broadcasted_iota(jnp.int32, cube, 2)
    line = lax.broadcasted_iota(jnp.int32, cube, 1)
    theta = heat[...] - AMBIENT_HEAT
    multiplier = of_kind(kind[...], factor)
    started = []
    for sweep in range(SWEEPS):
        cond = conductivity(theta + AMBIENT_HEAT, multiplier, nodes)
        pair = (theta, cond)
        for place, value in enumerate(pair):
            rows_out[sweep, 0, place] = value[:, 0, :]
            rows_out[sweep, 1, place] = value[:, rows - 1, :]
            turned = value.reshape(flat).T
            cols_out[sweep, 0, place : place + 1] = turned[:1]
            cols_out[sweep, 1, place : place + 1] = turned[width - 1 :]
        copies = []
        for side, shift in enumerate((-1, 1)):
            targets = (
                (cols_out, cols_in, (lax.rem(tx + shift + ntx, ntx), ty)),
                (rows_out, rows_in, (tx, lax.rem(ty + shift + nty, nty))),
            )
            for axis, (source, target, device) in enumerate(targets):
                copy = pltpu.make_async_remote_copy(
                    src_ref=source.at[sweep, side],
                    dst_ref=target.at[sweep, side],
                    send_sem=edge_send.at[sweep, side, axis],
                    recv_sem=edge_recv.at[sweep, side, axis],
                    device_id=device,
                    device_id_type=MESH,
                )
                copy.start()
                copies.append(copy)
        started += copies
        plane = laser_plane(rows, width, tx, ty, ntx, row_spots[sweep], col_spots[sweep])
        heating = jnp.stack([plane * math.exp(-sheet / LASER_DEPTH) for sheet in range(sheets)])
        vertical = 0.5 * (cond[1:] + cond[:-1]) * (theta[1:] - theta[:-1])
        zero_layer = jnp.zeros_like(theta[:1])
        flux = jnp.concatenate([vertical, zero_layer], 0) - jnp.concatenate(
            [zero_layer, vertical], 0
        )
        for copy in copies:
            copy.wait_recv()
        for side, shift in enumerate((-1, 1)):
            turned = cols_in[sweep, side].T
            edge = 0 if shift == 1 else width - 1
            other = []
            for place, value in enumerate(pair):
                moved = pltpu.roll(value.reshape(flat), shift % width, 1).reshape(cube)
                column = turned[:, place : place + 1].reshape(sheets, rows, 1)
                other.append(jnp.where(lane == edge, column, moved))
            flux = flux + 0.5 * (cond + other[1]) * (other[0] - theta)
            edge = 0 if shift == 1 else rows - 1
            inside = ty > 0 if shift == 1 else ty < nty - 1
            other = []
            for place, value in enumerate(pair):
                moved = pltpu.roll(value.reshape(flat), shift % flat[0], 0).reshape(cube)
                row = jnp.where(inside, rows_in[sweep, side, place], 0.0)
                other.append(jnp.where(line == edge, row[:, None, :], moved))
            flux = flux + 0.5 * (cond + other[1]) * (other[0] - theta)
        theta = theta + STEP_RATE * (flux + LASER_POWER * heating)
    return theta + AMBIENT_HEAT, started


def edge_scratch(sheets, rows, width):
    edge_rows = pltpu.VMEM((SWEEPS, 2, 2, sheets, width), jnp.float32)
    edge_cols = pltpu.VMEM((SWEEPS, 2, 8, sheets * rows), jnp.float32)
    sems = pltpu.SemaphoreType.DMA((SWEEPS, 2, 2))
    return [edge_rows, edge_rows, edge_cols, edge_cols, sems, sems]


def forward_kernel(
    ntx, nty, heat, kind, moment, nodes, factor, threshold, row_spots, col_spots, table_high,
    table_low, warmed, out, proportion, layered, gathered, left_high, left_low, blocks, rows_out,
    rows_in, cols_out, cols_in, edge_send, edge_recv, tx_send, tx_recv, ty_send, ty_recv,
):
    tx, ty = lax.axis_index("tx"), lax.axis_index("ty")
    parts, sheets, rows, width = moment.shape
    greet(tx, ty, ntx, nty)
    cols_out[...] = jnp.zeros_like(cols_out)
    state, edges = heat_sweeps(
        ntx, nty, heat, kind, nodes, factor, row_spots, col_spots, rows_out, rows_in, cols_out,
        cols_in, edge_send, edge_recv,
    )
    warmed[...] = state
    proportion[...] = jax.nn.sigmoid(
        (of_kind(kind[...], threshold) - state) * (1.0 / ORDERING_SPREAD)
    )
    count = 2 * sheets
    own = count // ntx
    tx_sems, ty_sems = (tx_send, tx_recv), (ty_send, ty_recv)

    def over_tx(step, part):
        return send_over("tx", step, part, layered, gathered, tx_sems, ntx, nty)

    def over_ty(step, part):
        return send_over("ty", step, part, blocks, out, ty_sems, ntx, nty)

    def layer_part(part, carry):
        for freq in range(sheets + 1):
            real = jnp.zeros((rows, width), jnp.float32)
            imag = jnp.zeros((rows, width), jnp.float32)
            for sheet in range(sheets):
                value = moment[part, sheet] * proportion[sheet]
                angle = 2.0 * math.pi * (sheet * freq % count) / count
                real = real + value * math.cos(angle)
                imag = imag - value * math.sin(angle)
            layered[freq // own, part, 0, freq % own] = real
            layered[freq // own, part, 1, freq % own] = imag
            if 0 < freq < sheets:
                other = count - freq
                layered[other // own, part, 0, other % own] = real
                layered[other // own, part, 1, other % own] = -imag
        return carry

    for part in range(parts):
        layer_part(part, 0)
        for step in range(1, ntx):
            over_tx(step, part).start()

    def transform(block, part):
        result = product(left_high[...], left_low[...], table_high[block], table_low[block])
        half = own * rows
        real = result[:half, :width] + result[half:, width:]
        imag = result[half:, :width] - result[:half, width:]
        return real.reshape(own, rows, width), imag.reshape(own, rows, width)

    def transform_part(part, carry):
        for step in range(1, ntx):
            over_tx(step, part).wait_recv()
        gathered[tx, part] = layered[tx, part]
        for source in range(ntx):
            high, low = split(gathered[source, part].reshape(2 * own * rows, width))
            left_high[:, source * width : (source + 1) * width] = high
            left_low[:, source * width : (source + 1) * width] = low

        def one(step, inner):
            block = lax.rem(ty + step, nty)
            real, imag = transform(block, part)
            blocks[block, part, :, :, :width] = real
            blocks[block, part, :, :, width:] = imag
            over_ty(step, part).start()
            return inner

        lax.fori_loop(1, nty, one, 0)
        real, imag = transform(ty, part)
        out[ty, part, :, :, :width] = real
        out[ty, part, :, :, width:] = imag
        return carry

    lax.fori_loop(0, parts, transform_part, 0)
    for edge in edges:
        edge.wait_send()
    for part in range(parts):
        for step in range(1, ntx):
            over_tx(step, part).wait_send()
        for step in range(1, nty):
            over_ty(step, part).wait()


def backward_kernel(
    ntx, nty, arrived, tensor_hbm, fwd_high, fwd_low, back_high, back_low, x_high_hbm, x_low_hbm,
    layers, out, tensor, x_high, x_low, spectra, field, returned, left_high, left_low, partial,
    landed, local_sem, ty_send, ty_recv, tx_send, tx_recv,
):
    tx, ty = lax.axis_index("tx"), lax.axis_index("ty")
    parts, own, rows = arrived.shape[1:4]
    width = arrived.shape[4] // 2
    total = nty * rows
    sheets = out.shape[1]
    tx_sems, ty_sems = (tx_send, tx_recv), (ty_send, ty_recv)
    loads = [
        pltpu.make_async_copy(tensor_hbm, tensor, local_sem.at[0]),
        pltpu.make_async_copy(x_high_hbm, x_high, local_sem.at[1]),
        pltpu.make_async_copy(x_low_hbm, x_low, local_sem.at[2]),
    ]
    for load in loads:
        load.start()

    def over_ty(step, part):
        return send_over("ty", step, part, field, returned, ty_sems, ntx, nty)

    def over_tx(step, part):
        return send_over("tx", step, part, partial, landed, tx_sems, ntx, nty)

    def forward_rows(index, carry):
        part, freq = index // own, index % own
        high, low = split(arrived[:, part, freq].reshape(total, 2 * width))
        result = product(fwd_high[...], fwd_low[...], high, low)
        half = 2 * total
        spectra[part, freq, :, :width] = result[:half, :width] + result[half:, width:]
        spectra[part, freq, :, width:] = result[:half, width:] - result[half:, :width]
        return carry

    lax.fori_loop(0, parts * own, forward_rows, 0)
    greet(tx, ty, ntx, nty)
    loads[0].wait()
    for part in range(parts):

        def back_rows(freq, carry):
            sides = []
            for side in range(2):
                lanes = slice(side * width, (side + 1) * width)
                sides.append(
                    tensor[PAIRS[part][0], freq] * spectra[0, freq, :, lanes]
                    + tensor[PAIRS[part][1], freq] * spectra[1, freq, :, lanes]
                    + tensor[PAIRS[part][2], freq] * spectra[2, freq, :, lanes]
                )
            high, low = split(jnp.concatenate(sides, axis=1))
            result = product(back_high[...], back_low[...], high, low)
            real = result[:total, :width] - result[total:, width:]
            imag = result[:total, width:] + result[total:, :width]
            field[:, part, 0, freq] = real.reshape(nty, rows, width)
            field[:, part, 1, freq] = imag.reshape(nty, rows, width)
            return carry

        lax.fori_loop(0, own, back_rows, 0)
        for step in range(1, nty):
            over_ty(step, part).start()
        returned[ty, part] = field[ty, part]
    loads[1].wait()
    loads[2].wait()

    def transform(block):
        result = product(left_high[...], left_low[...], x_high[block], x_low[block])
        half = own * rows
        real = result[:half, :width] - result[half:, width:]
        imag = result[:half, width:] + result[half:, :width]
        real, imag = real.reshape(own, rows, width), imag.reshape(own, rows, width)
        values = []
        for sheet in range(sheets):
            value = jnp.zeros((rows, width), jnp.float32)
            for freq in range(own):
                value = value + layers[tx * own + freq, 2 * sheet] * real[freq]
                value = value - layers[tx * own + freq, 2 * sheet + 1] * imag[freq]
            values.append(value)
        return values

    def inverse_part(part, carry):
        for step in range(1, nty):
            over_ty(step, part).wait_recv()
        for source in range(nty):
            high, low = split(returned[source, part].reshape(2 * own * rows, width))
            left_high[:, source * width : (source + 1) * width] = high
            left_low[:, source * width : (source + 1) * width] = low

        def one(step, inner):
            block = lax.rem(tx + step, ntx)
            for sheet, value in enumerate(transform(block)):
                partial[block, part, sheet] = value
            over_tx(step, part).start()
            return inner

        lax.fori_loop(1, ntx, one, 0)
        for sheet, value in enumerate(transform(tx)):
            landed[tx, part, sheet] = value
        return carry

    lax.fori_loop(0, parts, inverse_part, 0)
    for part in range(parts):
        for step in range(1, ntx):
            over_tx(step, part).wait_recv()
        total_field = landed[0, part]
        for source in range(1, ntx):
            total_field = total_field + landed[source, part]
        out[part] = total_field
    for part in range(parts):
        for step in range(1, nty):
            over_ty(step, part).wait_send()
        for step in range(1, ntx):
            over_tx(step, part).wait_send()


def vmem():
    return pl.BlockSpec(memory_space=pltpu.VMEM)


def params(identity):
    return pltpu.CompilerParams(
        collective_id=identity, has_side_effects=True, vmem_limit_bytes=60 * 1024 * 1024
    )


def spectra_over_rows(heat, kind, moment, scalars, ntx, nty):
    parts, sheets, rows, width = moment.shape
    own = 2 * sheets // ntx
    high, low = halves(blocked_pair(angles(ntx * width, nty * width, 2 * ntx * width), width))
    lines = 2 * own * rows
    dma = pltpu.SemaphoreType.DMA
    return pl.pallas_call(
        functools.partial(forward_kernel, ntx, nty),
        out_shape=(
            jax.ShapeDtypeStruct(heat.shape, jnp.float32),
            jax.ShapeDtypeStruct((nty, parts, own, rows, 2 * width), jnp.float32),
        ),
        in_specs=[vmem()] * 3
        + [pl.BlockSpec(memory_space=pltpu.SMEM)] * len(scalars)
        + [vmem()] * 2,
        out_specs=(vmem(), vmem()),
        scratch_shapes=[
            pltpu.VMEM((sheets, rows, width), jnp.float32),
            pltpu.VMEM((ntx, parts, 2, own, rows, width), jnp.float32),
            pltpu.VMEM((ntx, parts, 2, own, rows, width), jnp.float32),
            pltpu.VMEM((lines, ntx * width), jnp.bfloat16),
            pltpu.VMEM((lines, ntx * width), jnp.bfloat16),
            pltpu.VMEM((nty, parts, own, rows, 2 * width), jnp.float32),
            *edge_scratch(sheets, rows, width),
            dma((parts, ntx)),
            dma((parts, ntx)),
            dma((parts, nty)),
            dma((parts, nty)),
        ],
        compiler_params=params(0),
        name="forward_spectra",
    )(heat, kind, moment, *scalars, high, low)


def field_from_spectra(arrived, stray_tensor, sheets, ntx, nty):
    parts, own, rows = arrived.shape[1:4]
    width = arrived.shape[4] // 2
    total, columns = nty * rows, ntx * width
    count = 2 * sheets
    forward = angles(2 * total, total, 2 * total)
    forward = halves(np.concatenate([np.cos(forward), np.sin(forward)], axis=0))
    back = angles(total, 2 * total, 2 * total)
    back = halves(np.concatenate([np.cos(back), np.sin(back)], axis=0))
    x_table = halves(blocked_pair(angles(nty * width, columns, 2 * columns), width))
    turn = angles(count, sheets, count)
    scale = -1.0 / (count * 2 * total * 2 * columns)
    layers = np.stack([np.cos(turn), np.sin(turn)], axis=2).reshape(count, 2 * sheets) * scale
    lines = 2 * own * rows
    dma = pltpu.SemaphoreType.DMA
    anywhere = pl.BlockSpec(memory_space=pl.ANY)
    return pl.pallas_call(
        functools.partial(backward_kernel, ntx, nty),
        out_shape=jax.ShapeDtypeStruct((parts, sheets, rows, width), jnp.float32),
        in_specs=[vmem(), anywhere, vmem(), vmem(), vmem(), vmem(), anywhere, anywhere]
        + [pl.BlockSpec(memory_space=pltpu.SMEM)],
        out_specs=vmem(),
        scratch_shapes=[
            pltpu.VMEM(stray_tensor.shape, jnp.float32),
            pltpu.VMEM(x_table[0].shape, jnp.bfloat16),
            pltpu.VMEM(x_table[1].shape, jnp.bfloat16),
            pltpu.VMEM((parts, own, 2 * total, 2 * width), jnp.float32),
            pltpu.VMEM((nty, parts, 2, own, rows, width), jnp.float32),
            pltpu.VMEM((nty, parts, 2, own, rows, width), jnp.float32),
            pltpu.VMEM((lines, nty * width), jnp.bfloat16),
            pltpu.VMEM((lines, nty * width), jnp.bfloat16),
            pltpu.VMEM((ntx, parts, sheets, rows, width), jnp.float32),
            pltpu.VMEM((ntx, parts, sheets, rows, width), jnp.float32),
            dma((3,)),
            dma((parts, nty)),
            dma((parts, nty)),
            dma((parts, ntx)),
            dma((parts, ntx)),
        ],
        compiler_params=params(1),
        name="field_return",
    )(arrived, stray_tensor, *forward, *back, *x_table, layers.astype(np.float32))


def deep_table(table, axis):
    high, low = halves(table)
    return np.concatenate([high, low, high], axis=axis)


def deep_dot(table, high, low):
    data = jnp.concatenate([high, high, low], axis=0)
    return jnp.dot(table[...], data, preferred_element_type=jnp.float32)


def row_units(own, rows, cut):
    units = []
    for freq in range(own):
        pieces = 2 if freq == cut else 1
        lines = rows // pieces
        units += [(freq, piece * lines, lines) for piece in range(pieces)]
    return units


def flip(index, mask, size):
    result, bit = 0, 1
    while bit < size:
        result = result + (index // bit + mask // bit) % 2 * bit
        bit *= 2
    return result


def swapped(mask):
    return mask - mask % 8 + mask % 2 + mask // 2 % 2 * 4 + mask // 4 % 2 * 2


def mask_at(step, core, size):
    order = [2, 4, 3, 5, 6, 7, 1] if size == 8 else list(range(size - 1, 0, -1))
    mask = order[0]
    for place, value in enumerate(order):
        mask = jnp.where(step == place + 1, value, mask)
    return jnp.where(core == 0, mask, swapped(mask)) if size == 8 else mask


def send_rows(axis, step, unit, units, source, target, sems, ntx, nty):
    tx, ty = lax.axis_index("tx"), lax.axis_index("ty")
    freq, first, lines = units[unit]
    if axis == "tx":
        dest = lax.rem(tx + step, ntx)
        mine, device = tx, (dest, ty)
    else:
        dest = flip(ty, step, nty)
        mine, device = ty, (tx, dest)
    span = (slice(None),) * (len(source.shape) - 4) + (pl.ds(first, lines),)
    return pltpu.make_async_remote_copy(
        src_ref=source.at[(dest, freq) + span],
        dst_ref=target.at[(mine, freq) + span],
        send_sem=sems[0].at[unit, step],
        recv_sem=sems[1].at[unit, step],
        device_id=device,
        device_id_type=MESH,
    )


def settle(*values):
    def kernel(*refs):
        for index in range(len(values)):
            refs[len(values) + index][...] = refs[index][...]

    return pl.pallas_call(
        kernel,
        out_shape=tuple(jax.ShapeDtypeStruct(value.shape, value.dtype) for value in values),
        in_specs=[vmem()] * len(values),
        out_specs=(vmem(),) * len(values),
        name="settle",
    )(*values)


def whole_kernel(
    ntx, nty, heat, kind, nodes, factor, threshold, row_spots, col_spots, moment_hbm, to_hbm,
    forward_hbm, tensor_hbm, back_hbm, from_hbm, warmed, out, proportion, layered, gathered,
    blocks, arrived, spectra, field, returned, partial, landed, moment, to_table, forward_table,
    tensor, back_table, from_table, along_input, inverse_input, rows_out, rows_in, cols_out,
    cols_in, edge_send, edge_recv, local_sem, tx_send, tx_recv, ty_send, ty_recv, ty_back_send,
    ty_back_recv, tx_back_send, tx_back_recv,
):
    tx, ty = lax.axis_index("tx"), lax.axis_index("ty")
    parts, sheets, rows, width = moment.shape
    count = 2 * sheets
    own = count // ntx
    total = nty * rows
    ahead, behind = row_units(own, rows, 0), row_units(own, rows, own - 1)
    loads = [
        pltpu.make_async_copy(source, target, local_sem.at[index])
        for index, (source, target) in enumerate(
            (
                (moment_hbm, moment),
                (to_hbm, to_table),
                (forward_hbm, forward_table),
                (tensor_hbm, tensor),
                (back_hbm, back_table),
                (from_hbm, from_table),
            )
        )
    ]
    for load in loads:
        load.start()

    def tx_copy(step, unit):
        sems = (tx_send, tx_recv)
        return send_rows("tx", step, unit, ahead, layered, gathered, sems, ntx, nty)

    def ty_copy(step, unit):
        sems = (ty_send, ty_recv)
        return send_rows("ty", step, unit, ahead, blocks, arrived, sems, ntx, nty)

    def ty_return(step, unit):
        sems = (ty_back_send, ty_back_recv)
        return send_rows("ty", step, unit, behind, field, returned, sems, ntx, nty)

    def tx_return(step, unit):
        sems = (tx_back_send, tx_back_recv)
        return send_rows("tx", step, unit, behind, partial, landed, sems, ntx, nty)

    def start_all(copy, size, unit):
        for step in range(1, size):
            copy(step, unit).start()

    def await_all(copy, size, unit):
        for step in range(1, size):
            copy(step, unit).wait_recv()

    greet(tx, ty, ntx, nty)
    cols_out[...] = jnp.zeros_like(cols_out)
    state, edges = heat_sweeps(
        ntx, nty, heat, kind, nodes, factor, row_spots, col_spots, rows_out, rows_in, cols_out,
        cols_in, edge_send, edge_recv,
    )
    warmed[...] = state
    proportion[...] = jax.nn.sigmoid(
        (of_kind(kind[...], threshold) - state) * (1.0 / ORDERING_SPREAD)
    )

    def layer_spectra(freqs):
        def layer_part(part, carry):
            values = [moment[part, sheet] * proportion[sheet] for sheet in range(sheets)]
            for freq in freqs:
                real = jnp.zeros((rows, width), jnp.float32)
                imag = jnp.zeros((rows, width), jnp.float32)
                for sheet in range(sheets):
                    angle = 2.0 * math.pi * (sheet * freq % count) / count
                    real = real + values[sheet] * math.cos(angle)
                    imag = imag - values[sheet] * math.sin(angle)
                layered[freq // own, freq % own, 0, part] = real
                layered[freq // own, freq % own, 1, part] = imag
                if 0 < freq < sheets:
                    other = count - freq
                    layered[other // own, other % own, 0, part] = real
                    layered[other // own, other % own, 1, part] = -imag
            return carry

        lax.fori_loop(0, parts, layer_part, 0)

    loads[0].wait()
    ready = set()
    for freq in range(own):
        needed = []
        for line in range(sheets + 1):
            if line not in ready and freq in (line % own, (count - line) % own):
                needed.append(line)
        if needed:
            layer_spectra(needed)
            ready.update(needed)
        for unit in range(AHEAD):
            if ahead[unit][0] == freq:
                start_all(tx_copy, ntx, unit)

    def assemble(source, piece, size, target):
        freq, first, lines = piece
        depth = size * width
        for index in range(size):
            value = source[index, freq, :, :, first : first + lines]
            high, low = split(value.reshape(2 * parts * lines, width))
            for place, half in enumerate((high, high, low)):
                start = place * depth + index * width
                target[: 2 * parts * lines, start : start + width] = half

    def multiply(source, table, lines, sign):
        half = parts * lines
        result = jnp.dot(source[: 2 * half], table, preferred_element_type=jnp.float32)
        real = result[:half, :width] + sign * result[half:, width:]
        imag = result[half:, :width] - sign * result[:half, width:]
        return real.reshape(parts, lines, width), imag.reshape(parts, lines, width)

    def forward_columns(unit):
        freq, first, lines = ahead[unit]
        span = slice(first, first + lines)
        await_all(tx_copy, ntx, unit)
        if unit + AHEAD < len(ahead):
            start_all(tx_copy, ntx, unit + AHEAD)
        gathered[tx, freq, :, :, span] = layered[tx, freq, :, :, span]
        assemble(gathered, ahead[unit], ntx, along_input)
        if unit == 0:
            loads[1].wait()

        def one(step, carry):
            mask = mask_at(step, ty % 2, nty)
            block = flip(ty, mask, nty)
            real, imag = multiply(along_input, to_table[block], lines, 1.0)
            blocks[block, freq, :, span, :width] = real
            blocks[block, freq, :, span, width:] = imag
            ty_copy(mask, unit).start()
            return carry

        lax.fori_loop(1, nty, one, 0)
        real, imag = multiply(along_input, to_table[ty], lines, 1.0)
        arrived[ty, freq, :, span, :width] = real
        arrived[ty, freq, :, span, width:] = imag

    def through_rows(freq):
        for unit, piece in enumerate(ahead):
            if piece[0] == freq:
                await_all(ty_copy, nty, unit)
        if freq == 0:
            for load in loads[2:5]:
                load.wait()

        def forward_rows(part, carry):
            high, low = split(arrived[:, freq, part].reshape(total, 2 * width))
            result = deep_dot(forward_table, high, low)
            top = 2 * total
            spectra[part, :, :width] = result[:top, :width] + result[top:, width:]
            spectra[part, :, width:] = result[:top, width:] - result[top:, :width]
            return carry

        lax.fori_loop(0, parts, forward_rows, 0)
        for part in range(parts):
            sides = []
            for side in range(2):
                lanes = slice(side * width, (side + 1) * width)
                sides.append(
                    tensor[PAIRS[part][0], freq] * spectra[0, :, lanes]
                    + tensor[PAIRS[part][1], freq] * spectra[1, :, lanes]
                    + tensor[PAIRS[part][2], freq] * spectra[2, :, lanes]
                )
            high, low = split(jnp.concatenate(sides, axis=1))
            result = deep_dot(back_table, high, low)
            real = result[:total, :width] - result[total:, width:]
            imag = result[:total, width:] + result[total:, :width]
            field[:, freq, 0, part] = real.reshape(nty, rows, width)
            field[:, freq, 1, part] = imag.reshape(nty, rows, width)
        for unit, piece in enumerate(behind):
            if piece[0] == freq:
                for step in range(1, nty):
                    ty_return(mask_at(step, ty % 2, nty), unit).start()
        returned[ty, freq] = field[ty, freq]

    def inverse_columns(unit):
        freq, first, lines = behind[unit]
        span = slice(first, first + lines)
        await_all(ty_return, nty, unit)
        assemble(returned, behind[unit], nty, inverse_input)
        if unit == 0:
            loads[5].wait()

        def one(step, carry):
            block = lax.rem(tx + step, ntx)
            real, imag = multiply(inverse_input, from_table[block], lines, -1.0)
            partial[block, freq, 0, :, span] = real
            partial[block, freq, 1, :, span] = imag
            tx_return(step, unit).start()
            return carry

        lax.fori_loop(1, ntx, one, 0)
        real, imag = multiply(inverse_input, from_table[tx], lines, -1.0)
        landed[tx, freq, 0, :, span] = real
        landed[tx, freq, 1, :, span] = imag

    for turn in range(own + 3):
        for unit, piece in enumerate(ahead):
            if piece[0] == turn:
                forward_columns(unit)
        if 0 <= turn - 1 < own:
            through_rows(turn - 1)
        for unit, piece in enumerate(behind):
            if piece[0] == turn - 3:
                inverse_columns(unit)

    scale = -1.0 / (count * 2 * total * 2 * ntx * width)
    for unit, (freq, first, lines) in enumerate(behind):
        span = slice(first, first + lines)
        await_all(tx_return, ntx, unit)

        def back_layers(part, carry):
            for sheet in range(sheets):
                value = jnp.zeros((lines, width), jnp.float32)
                if freq > 0:
                    value = out[part, sheet, span]
                for source in range(ntx):
                    line = source * own + freq
                    angle = 2.0 * math.pi * (sheet * line % count) / count
                    value = value + landed[source, freq, 0, part, span] * (scale * math.cos(angle))
                    value = value - landed[source, freq, 1, part, span] * (scale * math.sin(angle))
                out[part, sheet, span] = value
            return carry

        lax.fori_loop(0, parts, back_layers, 0)

    for edge in edges:
        edge.wait_send()
    for unit in range(len(ahead)):
        for copy, size in ((tx_copy, ntx), (ty_copy, nty), (ty_return, nty), (tx_return, ntx)):
            for step in range(1, size):
                copy(step, unit).wait_send()


def everything(heat, kind, moment, stray_tensor, scalars, ntx, nty):
    parts, sheets, rows, width = moment.shape
    own = 2 * sheets // ntx
    total, columns = nty * rows, ntx * width
    forward = angles(2 * total, total, 2 * total)
    forward = deep_table(np.concatenate([np.cos(forward), np.sin(forward)], axis=0), 1)
    back = angles(total, 2 * total, 2 * total)
    back = deep_table(np.concatenate([np.cos(back), np.sin(back)], axis=0), 1)
    to_table = deep_table(blocked_pair(angles(columns, nty * width, 2 * columns), width), 1)
    from_table = deep_table(blocked_pair(angles(nty * width, columns, 2 * columns), width), 1)
    lines = 2 * parts * rows
    dma = pltpu.SemaphoreType.DMA
    anywhere = pl.BlockSpec(memory_space=pl.ANY)
    over_tx = pltpu.VMEM((ntx, own, 2, parts, rows, width), jnp.float32)
    over_ty = pltpu.VMEM((nty, own, parts, rows, 2 * width), jnp.float32)
    back_ty = pltpu.VMEM((nty, own, 2, parts, rows, width), jnp.float32)
    units = len(row_units(own, rows, 0))
    return settle(*pl.pallas_call(
        functools.partial(whole_kernel, ntx, nty),
        out_shape=(
            jax.ShapeDtypeStruct(heat.shape, jnp.float32),
            jax.ShapeDtypeStruct(moment.shape, jnp.float32),
        ),
        in_specs=[vmem()] * 2
        + [pl.BlockSpec(memory_space=pltpu.SMEM)] * len(scalars)
        + [anywhere] * 6,
        out_specs=(vmem(), vmem()),
        scratch_shapes=[
            pltpu.VMEM((sheets, rows, width), jnp.float32),
            over_tx,
            over_tx,
            over_ty,
            over_ty,
            pltpu.VMEM((parts, 2 * total, 2 * width), jnp.float32),
            back_ty,
            back_ty,
            over_tx,
            over_tx,
            pltpu.VMEM(moment.shape, jnp.float32),
            pltpu.VMEM(to_table.shape, jnp.bfloat16),
            pltpu.VMEM(forward.shape, jnp.bfloat16),
            pltpu.VMEM(stray_tensor.shape, jnp.float32),
            pltpu.VMEM(back.shape, jnp.bfloat16),
            pltpu.VMEM(from_table.shape, jnp.bfloat16),
            pltpu.VMEM((lines, 3 * columns), jnp.bfloat16),
            pltpu.VMEM((lines, 3 * nty * width), jnp.bfloat16),
            *edge_scratch(sheets, rows, width),
            dma((6,)),
            dma((units, ntx)),
            dma((units, ntx)),
            dma((units, nty)),
            dma((units, nty)),
            dma((units, nty)),
            dma((units, nty)),
            dma((units, ntx)),
            dma((units, ntx)),
        ],
        compiler_params=params(2),
        name="demagnetize",
    )(heat, kind, *scalars, moment, to_table, forward, stray_tensor, back, from_table))


def local(
    reduced_heat,
    substance_kind,
    moment_vector,
    stray_tensor,
    diffusivity_nodes,
    substance_factor,
    ordering_threshold,
    beam_transverse_spot,
    beam_downtrack_spot,
):
    ntx, nty = lax.axis_size("tx"), lax.axis_size("ty")
    scalars = (
        diffusivity_nodes,
        substance_factor,
        ordering_threshold,
        beam_transverse_spot,
        beam_downtrack_spot,
    )
    if 16 * ntx * nty * reduced_heat.shape[2] ** 2 <= TABLE_BYTES:
        return everything(
            reduced_heat, substance_kind, moment_vector, stray_tensor, scalars, ntx, nty
        )
    warmed_state, arrived = spectra_over_rows(
        reduced_heat, substance_kind, moment_vector, scalars, ntx, nty
    )
    demag_field = field_from_spectra(arrived, stray_tensor, reduced_heat.shape[0], ntx, nty)
    return (warmed_state, demag_field)


def solution(mesh):
    in_specs = (
        P(None, "ty", "tx"),
        P(None, "ty", "tx"),
        P(None, None, "ty", "tx"),
        P(None, "tx", None, "ty"),
        P(),
        P(),
        P(),
        P(),
        P(),
    )
    out_specs = (P(None, "ty", "tx"), P(None, None, "ty", "tx"))
    return jax.shard_map(local, mesh=mesh, in_specs=in_specs, out_specs=out_specs, check_vma=False)
```

```python
import functools
import math

import jax
import jax.numpy as jnp
import ml_dtypes
import numpy as np
from jax import lax
from jax.experimental import pallas as pl
from jax.experimental.pallas import tpu as pltpu
from jax.sharding import PartitionSpec as P

SWEEPS = 2


AMBIENT_HEAT = 0.3
STEP_RATE = 0.05
LASER_POWER = 4.0
LASER_DEPTH = 4.0
ORDERING_SPREAD = 0.08
TABLE_LOW = 0.2
TABLE_SPAN = 1.6


MESH = pl.DeviceIdType.MESH
AHEAD = 4
TABLE_BYTES = 16 * 1024 * 1024
PAIRS = ((0, 3, 4), (3, 1, 5), (4, 5, 2))


def halves(table):
    high = table.astype(ml_dtypes.bfloat16)
    low = (table - high.astype(np.float64)).astype(ml_dtypes.bfloat16)
    return (high, low)


def angles(rows, cols, length):
    grid = np.outer(np.arange(rows), np.arange(cols)) % length
    return grid * (2.0 * math.pi / length)


def blocked_pair(angle, width):
    rows, cols = angle.shape
    cosine = np.cos(angle).reshape(rows, cols // width, width)
    sine = np.sin(angle).reshape(rows, cols // width, width)
    return np.concatenate([cosine, sine], axis=2).transpose(1, 0, 2)


def split(value):
    high = value.astype(jnp.bfloat16)
    return (high, (value - high.astype(jnp.float32)).astype(jnp.bfloat16))


def product(left_high, left_low, right_high, right_low):
    def dot(a, b):
        return jnp.dot(a, b, preferred_element_type=jnp.float32)

    return dot(left_high, right_high) + (dot(left_high, right_low) + dot(left_low, right_high))


def greet(tx, ty, ntx, nty):
    barrier = pltpu.get_barrier_semaphore()
    for step in range(1, ntx):
        pl.semaphore_signal(
            barrier, inc=1, device_id=(lax.rem(tx + step, ntx), ty), device_id_type=MESH
        )
    for step in range(1, nty):
        pl.semaphore_signal(
            barrier, inc=1, device_id=(tx, lax.rem(ty + step, nty)), device_id_type=MESH
        )
    pl.semaphore_wait(barrier, ntx + nty - 2)


def send_over(axis, step, part, source, target, sems, ntx, nty):
    tx, ty = lax.axis_index("tx"), lax.axis_index("ty")
    if axis == "tx":
        dest = lax.rem(tx + step, ntx)
        mine, device = tx, (dest, ty)
    else:
        dest = lax.rem(ty + step, nty)
        mine, device = ty, (tx, dest)
    return pltpu.make_async_remote_copy(
        src_ref=source.at[dest, part],
        dst_ref=target.at[mine, part],
        send_sem=sems[0].at[part, step],
        recv_sem=sems[1].at[part, step],
        device_id=device,
        device_id_type=MESH,
    )


def conductivity(absolute, multiplier, nodes):
    count = nodes.shape[0]
    spacing = TABLE_SPAN / (count - 1)
    total = jnp.zeros_like(absolute) + nodes[0]
    for index in range(count - 1):
        place = (absolute - (TABLE_LOW + index * spacing)) * (1.0 / spacing)
        total = total + (nodes[index + 1] - nodes[index]) * jnp.clip(place, 0.0, 1.0)
    return multiplier * total


def of_kind(kind, values):
    result = jnp.zeros(kind.shape, jnp.float32)
    for grain in range(values.shape[0]):
        result = result + jnp.where(kind == grain, values[grain], 0.0)
    return result


def laser_plane(rows, width, tx, ty, ntx, row_spot, col_spot):
    total = ntx * width
    row_ids = lax.broadcasted_iota(jnp.int32, (rows, width), 0) + ty * rows
    col_ids = lax.broadcasted_iota(jnp.int32, (rows, width), 1) + tx * width
    along = col_ids - col_spot + total // 2
    along = jnp.where(along < 0, along + total, along)
    along = jnp.where(along >= total, along - total, along) - total // 2
    along = along.astype(jnp.float32) * (1.0 / (0.5 * width))
    across = (row_ids - row_spot).astype(jnp.float32) * (1.0 / rows)
    return jnp.exp(-0.5 * across * across) * jnp.exp(-0.5 * along * along)


def heat_sweeps(
    ntx, nty, heat, kind, nodes, factor, row_spots, col_spots, rows_out, rows_in, cols_out, cols_in,
    edge_send, edge_recv,
):
    tx, ty = lax.axis_index("tx"), lax.axis_index("ty")
    sheets, rows, width = heat.shape
    flat, cube = (sheets * rows, width), (sheets, rows, width)
    lane = lax.broadcasted_iota(jnp.int32, cube, 2)
    line = lax.broadcasted_iota(jnp.int32, cube, 1)
    theta = heat[...] - AMBIENT_HEAT
    multiplier = of_kind(kind[...], factor)
    started = []
    for sweep in range(SWEEPS):
        cond = conductivity(theta + AMBIENT_HEAT, multiplier, nodes)
        pair = (theta, cond)
        for place, value in enumerate(pair):
            rows_out[sweep, 0, place] = value[:, 0, :]
            rows_out[sweep, 1, place] = value[:, rows - 1, :]
            turned = value.reshape(flat).T
            cols_out[sweep, 0, place : place + 1] = turned[:1]
            cols_out[sweep, 1, place : place + 1] = turned[width - 1 :]
        copies = []
        for side, shift in enumerate((-1, 1)):
            targets = (
                (cols_out, cols_in, (lax.rem(tx + shift + ntx, ntx), ty)),
                (rows_out, rows_in, (tx, lax.rem(ty + shift + nty, nty))),
            )
            for axis, (source, target, device) in enumerate(targets):
                copy = pltpu.make_async_remote_copy(
                    src_ref=source.at[sweep, side],
                    dst_ref=target.at[sweep, side],
                    send_sem=edge_send.at[sweep, side, axis],
                    recv_sem=edge_recv.at[sweep, side, axis],
                    device_id=device,
                    device_id_type=MESH,
                )
                copy.start()
                copies.append(copy)
        started += copies
        plane = laser_plane(rows, width, tx, ty, ntx, row_spots[sweep], col_spots[sweep])
        heating = jnp.stack([plane * math.exp(-sheet / LASER_DEPTH) for sheet in range(sheets)])
        vertical = 0.5 * (cond[1:] + cond[:-1]) * (theta[1:] - theta[:-1])
        zero_layer = jnp.zeros_like(theta[:1])
        flux = jnp.concatenate([vertical, zero_layer], 0) - jnp.concatenate(
            [zero_layer, vertical], 0
        )
        for copy in copies:
            copy.wait_recv()
        for side, shift in enumerate((-1, 1)):
            turned = cols_in[sweep, side].T
            edge = 0 if shift == 1 else width - 1
            other = []
            for place, value in enumerate(pair):
                moved = pltpu.roll(value.reshape(flat), shift % width, 1).reshape(cube)
                column = turned[:, place : place + 1].reshape(sheets, rows, 1)
                other.append(jnp.where(lane == edge, column, moved))
            flux = flux + 0.5 * (cond + other[1]) * (other[0] - theta)
            edge = 0 if shift == 1 else rows - 1
            inside = ty > 0 if shift == 1 else ty < nty - 1
            other = []
            for place, value in enumerate(pair):
                moved = pltpu.roll(value.reshape(flat), shift % flat[0], 0).reshape(cube)
                row = jnp.where(inside, rows_in[sweep, side, place], 0.0)
                other.append(jnp.where(line == edge, row[:, None, :], moved))
            flux = flux + 0.5 * (cond + other[1]) * (other[0] - theta)
        theta = theta + STEP_RATE * (flux + LASER_POWER * heating)
    return theta + AMBIENT_HEAT, started


def edge_scratch(sheets, rows, width):
    edge_rows = pltpu.VMEM((SWEEPS, 2, 2, sheets, width), jnp.float32)
    edge_cols = pltpu.VMEM((SWEEPS, 2, 8, sheets * rows), jnp.float32)
    sems = pltpu.SemaphoreType.DMA((SWEEPS, 2, 2))
    return [edge_rows, edge_rows, edge_cols, edge_cols, sems, sems]


def forward_kernel(
    ntx, nty, heat, kind, moment, nodes, factor, threshold, row_spots, col_spots, table_high,
    table_low, warmed, out, proportion, layered, gathered, left_high, left_low, blocks, rows_out,
    rows_in, cols_out, cols_in, edge_send, edge_recv, tx_send, tx_recv, ty_send, ty_recv,
):
    tx, ty = lax.axis_index("tx"), lax.axis_index("ty")
    parts, sheets, rows, width = moment.shape
    greet(tx, ty, ntx, nty)
    cols_out[...] = jnp.zeros_like(cols_out)
    state, edges = heat_sweeps(
        ntx, nty, heat, kind, nodes, factor, row_spots, col_spots, rows_out, rows_in, cols_out,
        cols_in, edge_send, edge_recv,
    )
    warmed[...] = state
    proportion[...] = jax.nn.sigmoid(
        (of_kind(kind[...], threshold) - state) * (1.0 / ORDERING_SPREAD)
    )
    count = 2 * sheets
    own = count // ntx
    tx_sems, ty_sems = (tx_send, tx_recv), (ty_send, ty_recv)

    def over_tx(step, part):
        return send_over("tx", step, part, layered, gathered, tx_sems, ntx, nty)

    def over_ty(step, part):
        return send_over("ty", step, part, blocks, out, ty_sems, ntx, nty)

    def layer_part(part, carry):
        for freq in range(sheets + 1):
            real = jnp.zeros((rows, width), jnp.float32)
            imag = jnp.zeros((rows, width), jnp.float32)
            for sheet in range(sheets):
                value = moment[part, sheet] * proportion[sheet]
                angle = 2.0 * math.pi * (sheet * freq % count) / count
                real = real + value * math.cos(angle)
                imag = imag - value * math.sin(angle)
            layered[freq // own, part, 0, freq % own] = real
            layered[freq // own, part, 1, freq % own] = imag
            if 0 < freq < sheets:
                other = count - freq
                layered[other // own, part, 0, other % own] = real
                layered[other // own, part, 1, other % own] = -imag
        return carry

    for part in range(parts):
        layer_part(part, 0)
        for step in range(1, ntx):
            over_tx(step, part).start()

    def transform(block, part):
        result = product(left_high[...], left_low[...], table_high[block], table_low[block])
        half = own * rows
        real = result[:half, :width] + result[half:, width:]
        imag = result[half:, :width] - result[:half, width:]
        return real.reshape(own, rows, width), imag.reshape(own, rows, width)

    def transform_part(part, carry):
        for step in range(1, ntx):
            over_tx(step, part).wait_recv()
        gathered[tx, part] = layered[tx, part]
        for source in range(ntx):
            high, low = split(gathered[source, part].reshape(2 * own * rows, width))
            left_high[:, source * width : (source + 1) * width] = high
            left_low[:, source * width : (source + 1) * width] = low

        def one(step, inner):
            block = lax.rem(ty + step, nty)
            real, imag = transform(block, part)
            blocks[block, part, :, :, :width] = real
            blocks[block, part, :, :, width:] = imag
            over_ty(step, part).start()
            return inner

        lax.fori_loop(1, nty, one, 0)
        real, imag = transform(ty, part)
        out[ty, part, :, :, :width] = real
        out[ty, part, :, :, width:] = imag
        return carry

    lax.fori_loop(0, parts, transform_part, 0)
    for edge in edges:
        edge.wait_send()
    for part in range(parts):
        for step in range(1, ntx):
            over_tx(step, part).wait_send()
        for step in range(1, nty):
            over_ty(step, part).wait()


def backward_kernel(
    ntx, nty, arrived, tensor_hbm, fwd_high, fwd_low, back_high, back_low, x_high_hbm, x_low_hbm,
    layers, out, tensor, x_high, x_low, spectra, field, returned, left_high, left_low, partial,
    landed, local_sem, ty_send, ty_recv, tx_send, tx_recv,
):
    tx, ty = lax.axis_index("tx"), lax.axis_index("ty")
    parts, own, rows = arrived.shape[1:4]
    width = arrived.shape[4] // 2
    total = nty * rows
    sheets = out.shape[1]
    tx_sems, ty_sems = (tx_send, tx_recv), (ty_send, ty_recv)
    loads = [
        pltpu.make_async_copy(tensor_hbm, tensor, local_sem.at[0]),
        pltpu.make_async_copy(x_high_hbm, x_high, local_sem.at[1]),
        pltpu.make_async_copy(x_low_hbm, x_low, local_sem.at[2]),
    ]
    for load in loads:
        load.start()

    def over_ty(step, part):
        return send_over("ty", step, part, field, returned, ty_sems, ntx, nty)

    def over_tx(step, part):
        return send_over("tx", step, part, partial, landed, tx_sems, ntx, nty)

    def forward_rows(index, carry):
        part, freq = index // own, index % own
        high, low = split(arrived[:, part, freq].reshape(total, 2 * width))
        result = product(fwd_high[...], fwd_low[...], high, low)
        half = 2 * total
        spectra[part, freq, :, :width] = result[:half, :width] + result[half:, width:]
        spectra[part, freq, :, width:] = result[:half, width:] - result[half:, :width]
        return carry

    lax.fori_loop(0, parts * own, forward_rows, 0)
    greet(tx, ty, ntx, nty)
    loads[0].wait()
    for part in range(parts):

        def back_rows(freq, carry):
            sides = []
            for side in range(2):
                lanes = slice(side * width, (side + 1) * width)
                sides.append(
                    tensor[PAIRS[part][0], freq] * spectra[0, freq, :, lanes]
                    + tensor[PAIRS[part][1], freq] * spectra[1, freq, :, lanes]
                    + tensor[PAIRS[part][2], freq] * spectra[2, freq, :, lanes]
                )
            high, low = split(jnp.concatenate(sides, axis=1))
            result = product(back_high[...], back_low[...], high, low)
            real = result[:total, :width] - result[total:, width:]
            imag = result[:total, width:] + result[total:, :width]
            field[:, part, 0, freq] = real.reshape(nty, rows, width)
            field[:, part, 1, freq] = imag.reshape(nty, rows, width)
            return carry

        lax.fori_loop(0, own, back_rows, 0)
        for step in range(1, nty):
            over_ty(step, part).start()
        returned[ty, part] = field[ty, part]
    loads[1].wait()
    loads[2].wait()

    def transform(block):
        result = product(left_high[...], left_low[...], x_high[block], x_low[block])
        half = own * rows
        real = result[:half, :width] - result[half:, width:]
        imag = result[:half, width:] + result[half:, :width]
        real, imag = real.reshape(own, rows, width), imag.reshape(own, rows, width)
        values = []
        for sheet in range(sheets):
            value = jnp.zeros((rows, width), jnp.float32)
            for freq in range(own):
                value = value + layers[tx * own + freq, 2 * sheet] * real[freq]
                value = value - layers[tx * own + freq, 2 * sheet + 1] * imag[freq]
            values.append(value)
        return values

    def inverse_part(part, carry):
        for step in range(1, nty):
            over_ty(step, part).wait_recv()
        for source in range(nty):
            high, low = split(returned[source, part].reshape(2 * own * rows, width))
            left_high[:, source * width : (source + 1) * width] = high
            left_low[:, source * width : (source + 1) * width] = low

        def one(step, inner):
            block = lax.rem(tx + step, ntx)
            for sheet, value in enumerate(transform(block)):
                partial[block, part, sheet] = value
            over_tx(step, part).start()
            return inner

        lax.fori_loop(1, ntx, one, 0)
        for sheet, value in enumerate(transform(tx)):
            landed[tx, part, sheet] = value
        return carry

    lax.fori_loop(0, parts, inverse_part, 0)
    for part in range(parts):
        for step in range(1, ntx):
            over_tx(step, part).wait_recv()
        total_field = landed[0, part]
        for source in range(1, ntx):
            total_field = total_field + landed[source, part]
        out[part] = total_field
    for part in range(parts):
        for step in range(1, nty):
            over_ty(step, part).wait_send()
        for step in range(1, ntx):
            over_tx(step, part).wait_send()


def vmem():
    return pl.BlockSpec(memory_space=pltpu.VMEM)


def params(identity):
    return pltpu.CompilerParams(
        collective_id=identity, has_side_effects=True, vmem_limit_bytes=60 * 1024 * 1024
    )


def spectra_over_rows(heat, kind, moment, scalars, ntx, nty):
    parts, sheets, rows, width = moment.shape
    own = 2 * sheets // ntx
    high, low = halves(blocked_pair(angles(ntx * width, nty * width, 2 * ntx * width), width))
    lines = 2 * own * rows
    dma = pltpu.SemaphoreType.DMA
    return pl.pallas_call(
        functools.partial(forward_kernel, ntx, nty),
        out_shape=(
            jax.ShapeDtypeStruct(heat.shape, jnp.float32),
            jax.ShapeDtypeStruct((nty, parts, own, rows, 2 * width), jnp.float32),
        ),
        in_specs=[vmem()] * 3
        + [pl.BlockSpec(memory_space=pltpu.SMEM)] * len(scalars)
        + [vmem()] * 2,
        out_specs=(vmem(), vmem()),
        scratch_shapes=[
            pltpu.VMEM((sheets, rows, width), jnp.float32),
            pltpu.VMEM((ntx, parts, 2, own, rows, width), jnp.float32),
            pltpu.VMEM((ntx, parts, 2, own, rows, width), jnp.float32),
            pltpu.VMEM((lines, ntx * width), jnp.bfloat16),
            pltpu.VMEM((lines, ntx * width), jnp.bfloat16),
            pltpu.VMEM((nty, parts, own, rows, 2 * width), jnp.float32),
            *edge_scratch(sheets, rows, width),
            dma((parts, ntx)),
            dma((parts, ntx)),
            dma((parts, nty)),
            dma((parts, nty)),
        ],
        compiler_params=params(0),
        name="forward_spectra",
    )(heat, kind, moment, *scalars, high, low)


def field_from_spectra(arrived, stray_tensor, sheets, ntx, nty):
    parts, own, rows = arrived.shape[1:4]
    width = arrived.shape[4] // 2
    total, columns = nty * rows, ntx * width
    count = 2 * sheets
    forward = angles(2 * total, total, 2 * total)
    forward = halves(np.concatenate([np.cos(forward), np.sin(forward)], axis=0))
    back = angles(total, 2 * total, 2 * total)
    back = halves(np.concatenate([np.cos(back), np.sin(back)], axis=0))
    x_table = halves(blocked_pair(angles(nty * width, columns, 2 * columns), width))
    turn = angles(count, sheets, count)
    scale = -1.0 / (count * 2 * total * 2 * columns)
    layers = np.stack([np.cos(turn), np.sin(turn)], axis=2).reshape(count, 2 * sheets) * scale
    lines = 2 * own * rows
    dma = pltpu.SemaphoreType.DMA
    anywhere = pl.BlockSpec(memory_space=pl.ANY)
    return pl.pallas_call(
        functools.partial(backward_kernel, ntx, nty),
        out_shape=jax.ShapeDtypeStruct((parts, sheets, rows, width), jnp.float32),
        in_specs=[vmem(), anywhere, vmem(), vmem(), vmem(), vmem(), anywhere, anywhere]
        + [pl.BlockSpec(memory_space=pltpu.SMEM)],
        out_specs=vmem(),
        scratch_shapes=[
            pltpu.VMEM(stray_tensor.shape, jnp.float32),
            pltpu.VMEM(x_table[0].shape, jnp.bfloat16),
            pltpu.VMEM(x_table[1].shape, jnp.bfloat16),
            pltpu.VMEM((parts, own, 2 * total, 2 * width), jnp.float32),
            pltpu.VMEM((nty, parts, 2, own, rows, width), jnp.float32),
            pltpu.VMEM((nty, parts, 2, own, rows, width), jnp.float32),
            pltpu.VMEM((lines, nty * width), jnp.bfloat16),
            pltpu.VMEM((lines, nty * width), jnp.bfloat16),
            pltpu.VMEM((ntx, parts, sheets, rows, width), jnp.float32),
            pltpu.VMEM((ntx, parts, sheets, rows, width), jnp.float32),
            dma((3,)),
            dma((parts, nty)),
            dma((parts, nty)),
            dma((parts, ntx)),
            dma((parts, ntx)),
        ],
        compiler_params=params(1),
        name="field_return",
    )(arrived, stray_tensor, *forward, *back, *x_table, layers.astype(np.float32))


def whole_kernel(
    ntx, nty, heat, kind, moment, nodes, factor, threshold, row_spots, col_spots, fwd_high, fwd_low,
    back_high, back_low, tensor_hbm, to_high_hbm, to_low_hbm, from_high_hbm, from_low_hbm,
    warmed, out, proportion, layered, gathered, blocks, arrived, spectra, field, returned, partial,
    landed, tensor, to_high, to_low, from_high, from_low, along_high, along_low, inverse_high,
    inverse_low, rows_out, rows_in, cols_out, cols_in, edge_send, edge_recv, local_sem, tx_send,
    tx_recv, ty_send, ty_recv, ty_back_send, ty_back_recv, tx_back_send, tx_back_recv,
):
    tx, ty = lax.axis_index("tx"), lax.axis_index("ty")
    parts, sheets, rows, width = moment.shape
    count = 2 * sheets
    own = count // ntx
    total = nty * rows
    half = parts * rows
    loads = [
        pltpu.make_async_copy(source, target, local_sem.at[index])
        for index, (source, target) in enumerate(
            (
                (to_high_hbm, to_high),
                (to_low_hbm, to_low),
                (tensor_hbm, tensor),
                (from_high_hbm, from_high),
                (from_low_hbm, from_low),
            )
        )
    ]
    for load in loads:
        load.start()

    def tx_copy(step, freq):
        sems = (tx_send, tx_recv)
        return send_over("tx", step, freq, layered, gathered, sems, ntx, nty)

    def ty_copy(step, freq):
        return send_over("ty", step, freq, blocks, arrived, (ty_send, ty_recv), ntx, nty)

    def ty_return(step, freq):
        sems = (ty_back_send, ty_back_recv)
        return send_over("ty", step, freq, field, returned, sems, ntx, nty)

    def tx_return(step, freq):
        sems = (tx_back_send, tx_back_recv)
        return send_over("tx", step, freq, partial, landed, sems, ntx, nty)

    def start_all(copy, size, freq):
        for step in range(1, size):
            copy(step, freq).start()

    def await_all(copy, size, freq):
        for step in range(1, size):
            copy(step, freq).wait_recv()

    greet(tx, ty, ntx, nty)
    cols_out[...] = jnp.zeros_like(cols_out)
    state, edges = heat_sweeps(
        ntx, nty, heat, kind, nodes, factor, row_spots, col_spots, rows_out, rows_in, cols_out,
        cols_in, edge_send, edge_recv,
    )
    warmed[...] = state
    proportion[...] = jax.nn.sigmoid(
        (of_kind(kind[...], threshold) - state) * (1.0 / ORDERING_SPREAD)
    )

    def layer_spectra(freqs):
        def layer_part(part, carry):
            values = [moment[part, sheet] * proportion[sheet] for sheet in range(sheets)]
            for freq in freqs:
                real = jnp.zeros((rows, width), jnp.float32)
                imag = jnp.zeros((rows, width), jnp.float32)
                for sheet in range(sheets):
                    angle = 2.0 * math.pi * (sheet * freq % count) / count
                    real = real + values[sheet] * math.cos(angle)
                    imag = imag - values[sheet] * math.sin(angle)
                layered[freq // own, freq % own, 0, part] = real
                layered[freq // own, freq % own, 1, part] = imag
                if 0 < freq < sheets:
                    other = count - freq
                    layered[other // own, other % own, 0, part] = real
                    layered[other // own, other % own, 1, part] = -imag
            return carry

        lax.fori_loop(0, parts, layer_part, 0)

    ready = set()
    for freq in range(own):
        needed = []
        for line in range(sheets + 1):
            if line not in ready and freq in (line % own, (count - line) % own):
                needed.append(line)
        if needed:
            layer_spectra(needed)
            ready.update(needed)
        if freq < min(AHEAD, own):
            start_all(tx_copy, ntx, freq)

    def assemble(source, freq, size, high_ref, low_ref):
        for index in range(size):
            high, low = split(source[index, freq].reshape(2 * half, width))
            high_ref[:, index * width : (index + 1) * width] = high
            low_ref[:, index * width : (index + 1) * width] = low

    def along(block):
        result = product(along_high[...], along_low[...], to_high[block], to_low[block])
        real = result[:half, :width] + result[half:, width:]
        imag = result[half:, :width] - result[:half, width:]
        return real.reshape(parts, rows, width), imag.reshape(parts, rows, width)

    def forward_columns(freq):
        await_all(tx_copy, ntx, freq)
        if freq + AHEAD < own:
            start_all(tx_copy, ntx, freq + AHEAD)
        gathered[tx, freq] = layered[tx, freq]
        assemble(gathered, freq, ntx, along_high, along_low)
        if freq == 0:
            loads[0].wait()
            loads[1].wait()

        def one(step, carry):
            block = lax.rem(ty + step, nty)
            real, imag = along(block)
            blocks[block, freq, :, :, :width] = real
            blocks[block, freq, :, :, width:] = imag
            ty_copy(step, freq).start()
            return carry

        lax.fori_loop(1, nty, one, 0)
        real, imag = along(ty)
        arrived[ty, freq, :, :, :width] = real
        arrived[ty, freq, :, :, width:] = imag

    def through_rows(freq):
        await_all(ty_copy, nty, freq)

        def forward_rows(part, carry):
            high, low = split(arrived[:, freq, part].reshape(total, 2 * width))
            result = product(fwd_high[...], fwd_low[...], high, low)
            top = 2 * total
            spectra[part, :, :width] = result[:top, :width] + result[top:, width:]
            spectra[part, :, width:] = result[:top, width:] - result[top:, :width]
            return carry

        lax.fori_loop(0, parts, forward_rows, 0)
        if freq == 0:
            loads[2].wait()
        for part in range(parts):
            sides = []
            for side in range(2):
                lanes = slice(side * width, (side + 1) * width)
                sides.append(
                    tensor[PAIRS[part][0], freq] * spectra[0, :, lanes]
                    + tensor[PAIRS[part][1], freq] * spectra[1, :, lanes]
                    + tensor[PAIRS[part][2], freq] * spectra[2, :, lanes]
                )
            high, low = split(jnp.concatenate(sides, axis=1))
            result = product(back_high[...], back_low[...], high, low)
            real = result[:total, :width] - result[total:, width:]
            imag = result[:total, width:] + result[total:, :width]
            field[:, freq, 0, part] = real.reshape(nty, rows, width)
            field[:, freq, 1, part] = imag.reshape(nty, rows, width)
        start_all(ty_return, nty, freq)
        returned[ty, freq] = field[ty, freq]

    def inverse(block):
        result = product(inverse_high[...], inverse_low[...], from_high[block], from_low[block])
        real = result[:half, :width] - result[half:, width:]
        imag = result[:half, width:] + result[half:, :width]
        return real.reshape(parts, rows, width), imag.reshape(parts, rows, width)

    def inverse_columns(freq):
        await_all(ty_return, nty, freq)
        assemble(returned, freq, nty, inverse_high, inverse_low)
        if freq == 0:
            loads[3].wait()
            loads[4].wait()

        def one(step, carry):
            block = lax.rem(tx + step, ntx)
            partial[block, freq, 0], partial[block, freq, 1] = inverse(block)
            tx_return(step, freq).start()
            return carry

        lax.fori_loop(1, ntx, one, 0)
        landed[tx, freq, 0], landed[tx, freq, 1] = inverse(tx)

    for turn in range(own + 3):
        if turn < own:
            forward_columns(turn)
        if 0 <= turn - 1 < own:
            through_rows(turn - 1)
        if 0 <= turn - 3 < own:
            inverse_columns(turn - 3)

    scale = -1.0 / (count * 2 * total * 2 * ntx * width)
    for freq in range(own):
        await_all(tx_return, ntx, freq)

        def back_layers(part, carry):
            for sheet in range(sheets):
                value = jnp.zeros((rows, width), jnp.float32) if freq == 0 else out[part, sheet]
                for source in range(ntx):
                    line = source * own + freq
                    angle = 2.0 * math.pi * (sheet * line % count) / count
                    value = value + landed[source, freq, 0, part] * (scale * math.cos(angle))
                    value = value - landed[source, freq, 1, part] * (scale * math.sin(angle))
                out[part, sheet] = value
            return carry

        lax.fori_loop(0, parts, back_layers, 0)

    for edge in edges:
        edge.wait_send()
    for freq in range(own):
        for copy, size in ((tx_copy, ntx), (ty_copy, nty), (ty_return, nty), (tx_return, ntx)):
            for step in range(1, size):
                copy(step, freq).wait_send()


def settle(*values):
    def kernel(*refs):
        for index in range(len(values)):
            refs[len(values) + index][...] = refs[index][...]

    return pl.pallas_call(
        kernel,
        out_shape=tuple(jax.ShapeDtypeStruct(value.shape, value.dtype) for value in values),
        in_specs=[vmem()] * len(values),
        out_specs=(vmem(),) * len(values),
        name="settle",
    )(*values)


def everything(heat, kind, moment, stray_tensor, scalars, ntx, nty):
    parts, sheets, rows, width = moment.shape
    own = 2 * sheets // ntx
    total, columns = nty * rows, ntx * width
    forward = angles(2 * total, total, 2 * total)
    forward = halves(np.concatenate([np.cos(forward), np.sin(forward)], axis=0))
    back = angles(total, 2 * total, 2 * total)
    back = halves(np.concatenate([np.cos(back), np.sin(back)], axis=0))
    to_table = halves(blocked_pair(angles(columns, nty * width, 2 * columns), width))
    from_table = halves(blocked_pair(angles(nty * width, columns, 2 * columns), width))
    lines = 2 * parts * rows
    dma = pltpu.SemaphoreType.DMA
    anywhere = pl.BlockSpec(memory_space=pl.ANY)
    over_tx = pltpu.VMEM((ntx, own, 2, parts, rows, width), jnp.float32)
    over_ty = pltpu.VMEM((nty, own, parts, rows, 2 * width), jnp.float32)
    back_ty = pltpu.VMEM((nty, own, 2, parts, rows, width), jnp.float32)
    return settle(*pl.pallas_call(
        functools.partial(whole_kernel, ntx, nty),
        out_shape=(
            jax.ShapeDtypeStruct(heat.shape, jnp.float32),
            jax.ShapeDtypeStruct(moment.shape, jnp.float32),
        ),
        in_specs=[vmem()] * 3
        + [pl.BlockSpec(memory_space=pltpu.SMEM)] * len(scalars)
        + [vmem()] * 4
        + [anywhere] * 5,
        out_specs=(vmem(), vmem()),
        scratch_shapes=[
            pltpu.VMEM((sheets, rows, width), jnp.float32),
            over_tx,
            over_tx,
            over_ty,
            over_ty,
            pltpu.VMEM((parts, 2 * total, 2 * width), jnp.float32),
            back_ty,
            back_ty,
            over_tx,
            over_tx,
            pltpu.VMEM(stray_tensor.shape, jnp.float32),
            pltpu.VMEM(to_table[0].shape, jnp.bfloat16),
            pltpu.VMEM(to_table[1].shape, jnp.bfloat16),
            pltpu.VMEM(from_table[0].shape, jnp.bfloat16),
            pltpu.VMEM(from_table[1].shape, jnp.bfloat16),
            pltpu.VMEM((lines, columns), jnp.bfloat16),
            pltpu.VMEM((lines, columns), jnp.bfloat16),
            pltpu.VMEM((lines, nty * width), jnp.bfloat16),
            pltpu.VMEM((lines, nty * width), jnp.bfloat16),
            *edge_scratch(sheets, rows, width),
            dma((5,)),
            dma((own, ntx)),
            dma((own, ntx)),
            dma((own, nty)),
            dma((own, nty)),
            dma((own, nty)),
            dma((own, nty)),
            dma((own, ntx)),
            dma((own, ntx)),
        ],
        compiler_params=params(2),
        name="demagnetize",
    )(heat, kind, moment, *scalars, *forward, *back, stray_tensor, *to_table, *from_table))


def local(
    reduced_heat,
    substance_kind,
    moment_vector,
    stray_tensor,
    diffusivity_nodes,
    substance_factor,
    ordering_threshold,
    beam_transverse_spot,
    beam_downtrack_spot,
):
    ntx, nty = lax.axis_size("tx"), lax.axis_size("ty")
    scalars = (
        diffusivity_nodes,
        substance_factor,
        ordering_threshold,
        beam_transverse_spot,
        beam_downtrack_spot,
    )
    if 16 * ntx * nty * reduced_heat.shape[2] ** 2 <= TABLE_BYTES:
        return everything(
            reduced_heat, substance_kind, moment_vector, stray_tensor, scalars, ntx, nty
        )
    warmed_state, arrived = spectra_over_rows(
        reduced_heat, substance_kind, moment_vector, scalars, ntx, nty
    )
    demag_field = field_from_spectra(arrived, stray_tensor, reduced_heat.shape[0], ntx, nty)
    return (warmed_state, demag_field)


def solution(mesh):
    in_specs = (
        P(None, "ty", "tx"),
        P(None, "ty", "tx"),
        P(None, None, "ty", "tx"),
        P(None, "tx", None, "ty"),
        P(),
        P(),
        P(),
        P(),
        P(),
    )
    out_specs = (P(None, "ty", "tx"), P(None, None, "ty", "tx"))
    return jax.shard_map(local, mesh=mesh, in_specs=in_specs, out_specs=out_specs, check_vma=False)
```
